256 devices in a mesh: dp: 8 (over y_hi, x), tensor: 32 (over y_lo, z, core).
Axes of the slice: x: 4, y: 4 (y_hi: 2, y_lo: 2; y = y_hi * 2 + y_lo), z: 8, core: 2. Of those that a mesh axis runs over, the one named last changes fastest.
Arguments:
- query: bfloat16 [4096, 8192], P('dp', 'tensor'), parts along dimension 0, may hold values from -72 to 72
- keys: bfloat16 [4096, 1024], P('dp'), parts along dimension 0, may hold values from -4 to 4
- values: bfloat16 [4096, 1024], P('dp'), parts along dimension 0, may hold values from -5 to 5
- out_weight: bfloat16 [8192, 8192], P('tensor'), may hold values from -0.0625 to 0.0625
- scale_exp: int32 [32, 4096, 64], P('tensor', 'dp'), parts along dimension 1, may hold values from -13 to -7
- residual: bfloat16 [4096, 8192], P(('dp', 'tensor')), parts along dimension 0, may hold values from -2 to 2
- norm_gain: bfloat16 [8192], replicated, may hold values from 0.25 to 1.75
- next_weight: bfloat16 [8192, 8192], P(None, 'tensor'), may hold values from -0.0625 to 0.0625
- doc_lengths: int32 [32], P('dp'), parts along dimension 0, may hold values from 1 to 256, 512 in all
Outputs:
- next_query: bfloat16 [4096, 8192], P('dp', 'tensor'), parts along dimension 0
- residual_out: bfloat16 [4096, 8192], P(('dp', 'tensor')), parts along dimension 0
The draws below stay inside these ranges and needn't reach their ends.
There are 8 independent parts, one for each index of `dp`. The reference program is written for one: setup_inputs(seed, part) draws one part's arguments, and reference() takes and returns one part's arrays. A program takes and returns all parts, laid end to end along the dimension named above; an argument that names none is the same for every part. Nothing has to cross between parts.
Inputs may be any that keep to these rules, and one draw needn't show every extreme that they name: `doc_lengths`: the 4 lengths sum to 512; the longest has exactly 256 tokens.
All inputs are finite; a program needn't handle non-finite values.
Results may differ from the reference program's by a relative error of at most 0.024.
Values may be sent and summed in bfloat16 or wider, within the bound.
No kernel may reach another device: no remote copies, remote signals or barrier semaphores. Data moves between devices by JAX's collectives and lax.ppermute only.
A program may use at most 128 MiB of HBM per device.

```python
import math
import jax
import jax.numpy as jnp
import numpy as np
from jax import lax

D = 8192
HD = 128
HEADS_DEV = 2
KV_HEADS = 8
TOK = 512
DOCS = 4
Q_HEADS = 64
MOST = 256
N_TENSOR = 32


def shared_keys(key):
    return jnp.clip(jax.random.normal(key, (TOK, KV_HEADS * HD), jnp.float32), -4.0, 4.0)


def draw_keys(key, part):
    base = shared_keys(key)
    return base.astype(jnp.bfloat16)


def draw_query(key, part):
    key = jax.random.fold_in(key, 11)
    drawn = jnp.clip(jax.random.normal(key, (TOK, Q_HEADS * HD), jnp.float32), -4.0, 4.0)
    return drawn.astype(jnp.bfloat16)


def set_ends(array, own_key, smallest, high):
    shape = array.shape
    place = [jax.random.randint(jax.random.fold_in(own_key, axis), (), 0, shape[axis]) for axis in range(len(shape))]
    array = array.at[tuple(place)].set(smallest)
    longest = shape.index(max(shape))
    place[longest] = (place[longest] + 1) % shape[longest]
    return array.at[tuple(place)].set(high)


def block_levels(key, dims, split, least, top_value):
    def one(dim, parts):
        heights = jax.random.uniform(jax.random.fold_in(jax.random.fold_in(key, 6), dim), (parts,), jnp.float32, least / len(split), top_value / len(split))
        return jnp.repeat(jnp.exp(heights), dims[dim] // parts).reshape((-1,) + (1,) * (len(dims) - dim - 1))

    loudness = one(*split[0])
    for cut in split[1:]:
        loudness = loudness * one(*cut)
    return loudness


def length_profile(number_of, total, limit, slope):
    portions = [(1 << 20) // math.isqrt(rank ** slope) + 1 for rank in range(2, number_of + 1)]
    rest, given = total - limit - (number_of - 1), [1] * (number_of - 1)
    while rest > 0:
        movable = [i for i in range(number_of - 1) if given[i] < limit]
        pool, budget = sum([portions[i] for i in movable]), rest
        for i in movable:
            extra = min(limit - given[i], max(1, budget * portions[i] // pool), rest)
            given[i] = given[i] + extra
            rest = rest - extra
    return np.array([limit] + given)


def uneven_parts(own_key, amount, total, reach, lean):
    if amount == 2:
        one = jax.random.randint(own_key, (), max(1, total - reach), min(reach, total - 1) + 1)
        return jnp.stack([one, total - one])
    sizes = jnp.asarray(length_profile(amount, total, reach, lean), jnp.int32)
    pairs = (amount - 1) // 2
    giver, receiver = sizes[1:1 + 2 * pairs:2], sizes[2:2 + 2 * pairs:2]
    room = jnp.minimum(giver - 1, reach - receiver)
    passed = jax.random.randint(jax.random.fold_in(own_key, 1), (pairs,), 0, 1 << 20) % (room + 1)
    sizes = sizes.at[1:1 + 2 * pairs:2].set(giver - passed).at[2:2 + 2 * pairs:2].set(receiver + passed)
    return sizes[jax.random.permutation(jax.random.fold_in(own_key, 2), amount)]


def normal_values(stream_key, extent, deviation, limit, split=(), held_as=jnp.bfloat16):
    drawn = jax.random.normal(stream_key, extent, jnp.float32) * deviation
    if len(split) > 0:
        drawn = block_levels(stream_key, extent, split, -0.22, 0.18) * drawn
    return jnp.clip(drawn, min=-limit, max=limit).astype(held_as)


def setup_inputs(seed: int = 0, part: int = 0) -> dict:
    splits = jax.random.split(jax.random.key(seed), 10)
    part_splits = jax.random.split(jax.random.fold_in(splits[9], part), 10)
    return {
        "query": draw_query(jax.random.fold_in(jax.random.fold_in(splits[9], part), 71), part),
        "keys": draw_keys(jax.random.fold_in(jax.random.fold_in(splits[9], part), 71), part),
        "values": normal_values(part_splits[2], (TOK, KV_HEADS * HD), 1.0, 5.0),
        "out_weight": normal_values(splits[3], (Q_HEADS * HD, D), (Q_HEADS * HD) ** -0.5, 0.0625, ((0, 32),)),
        "scale_exp": set_ends(jax.random.randint(part_splits[4], (N_TENSOR, TOK, D // 128), -13, -6), jax.random.fold_in(part_splits[4], 1), -13, (-6) - 1).astype(jnp.int32),
        "residual": normal_values(part_splits[5], (TOK, D), 0.3, 2.0, ((0, 32),)),
        "norm_gain": jnp.clip(1.0 + 0.15 * jax.random.normal(splits[6], (D,), jnp.float32), 0.25, 1.75).astype(jnp.bfloat16),
        "next_weight": normal_values(splits[7], (D, Q_HEADS * HD), D ** -0.5, 0.0625, ((1, 32),)),
        "doc_lengths": uneven_parts(part_splits[8], DOCS, TOK, MOST, 1).astype(jnp.int32),
    }


def hadamard_table():
    index = jnp.arange(128, dtype=jnp.int32)
    joined = index[:, None] & index[None, :]
    parity = jnp.zeros((128, 128), jnp.int32)
    for shift in range(7):
        parity = parity + (joined >> shift & 1)
    signs = 1 - 2 * (parity % 2)
    return signs.astype(jnp.float32) / math.sqrt(128.0)

def power_table(expo, sign):
    result = jnp.zeros(expo.shape, jnp.float32)
    for level in range(-13, -6):
        result = result + jnp.where(expo == level, jnp.float32(2.0 ** (sign * level)), jnp.float32(0.0))
    return result

def rotate_blocks(field):
    count = field.shape[0]
    blocks = field.reshape(count, -1, 128)
    turned = jnp.einsum('rbi,ij->rbj', blocks, hadamard_table(), precision=lax.Precision.HIGHEST)
    return turned.reshape(count, -1)

def quantize_term(partial_value, expo):
    count = partial_value.shape[0]
    turned = rotate_blocks(partial_value).reshape(count, -1, 128)
    scaled = jnp.clip(turned * power_table(expo, -1)[:, :, None], -448.0, 448.0)
    coded = lax.optimization_barrier(scaled.astype(jnp.bfloat16))
    return (coded.astype(jnp.float32) * power_table(expo, 1)[:, :, None]).reshape(count, -1)

def segment_ids(doc_lengths, count):
    ends = jnp.cumsum(doc_lengths).astype(jnp.int32)
    position = jnp.arange(count, dtype=jnp.int32)
    return lax.optimization_barrier(jnp.sum((position[:, None] >= ends[None, :]).astype(jnp.int32), axis=1))

def attend_head(q_head, k_head, v_head, q_pos, q_seg, k_pos, k_seg):
    scores = jnp.dot(q_head, k_head.T, preferred_element_type=jnp.float32) * HD ** (-0.5)
    allowed = (k_seg[None, :] == q_seg[:, None]) & (k_pos[None, :] <= q_pos[:, None])
    scores = jnp.where(allowed, scores, jnp.float32(-1e+30))
    top = lax.optimization_barrier(jnp.max(scores, axis=1, keepdims=True))
    expo = jnp.where(allowed, jnp.exp(scores - top), jnp.float32(0.0))
    probs = (expo / lax.optimization_barrier(jnp.sum(expo, axis=1, keepdims=True))).astype(jnp.bfloat16)
    return jnp.dot(probs, v_head, preferred_element_type=jnp.float32).astype(jnp.bfloat16)

def reference(query, keys, values, out_weight, scale_exp, residual, norm_gain, next_weight, doc_lengths):
    segment = segment_ids(doc_lengths, TOK)
    position = jnp.arange(TOK, dtype=jnp.int32)
    group = Q_HEADS // KV_HEADS

    def one_head(head):
        q_head = lax.dynamic_slice_in_dim(query, (head * HD).astype(jnp.int32), HD, 1)
        start = (head // group * HD).astype(jnp.int32)
        k_head = lax.dynamic_slice_in_dim(keys, start, HD, 1)
        v_head = lax.dynamic_slice_in_dim(values, start, HD, 1)
        return attend_head(q_head, k_head, v_head, position, segment, position, segment)
    heads = lax.map(one_head, jnp.arange(Q_HEADS, dtype=jnp.int32))
    attn = heads.transpose(1, 0, 2).reshape(TOK, Q_HEADS * HD)
    width = HEADS_DEV * HD

    def add_device(device, total):
        start = (device * width).astype(jnp.int32)
        rows = lax.dynamic_slice_in_dim(attn, start, width, 1)
        weight = lax.dynamic_slice_in_dim(out_weight, start, width, 0)
        partial_value = jnp.dot(rows, weight, preferred_element_type=jnp.float32)
        expo = lax.dynamic_index_in_dim(scale_exp, device, 0, keepdims=False)
        return total + quantize_term(partial_value, expo)
    total = lax.fori_loop(0, N_TENSOR, add_device, jnp.zeros((TOK, D), jnp.float32))
    updated = residual.astype(jnp.float32) + rotate_blocks(total)
    inverse = lax.rsqrt(lax.optimization_barrier(jnp.mean(updated * updated, axis=1, keepdims=True)) + 1e-05)
    normed = (updated * inverse * norm_gain.astype(jnp.float32)).astype(jnp.bfloat16)
    next_query = jnp.dot(normed, next_weight, preferred_element_type=jnp.float32).astype(jnp.bfloat16)
    return (next_query, updated.astype(jnp.bfloat16))
```

```python
import functools
import math

import jax
import jax.numpy as jnp
from jax import lax
from jax.experimental import pallas as pl
from jax.experimental.pallas import tpu as pltpu
from jax.sharding import PartitionSpec as P

HD = 128
KV_HEADS = 8
LEVELS = range(-13, -6)
F32 = jnp.float32
BF16 = jnp.bfloat16

NY, NZ, NC = 2, 8, 2


def moves(step):
    def index(y, z, c):
        return (y * NZ + z) * NC + c

    return [
        (index(y, z, c), index(*step(y, z, c)))
        for y in range(NY)
        for z in range(NZ)
        for c in range(NC)
    ]


Z_UP = moves(lambda y, z, c: (y, (z + 1) % NZ, c))
Z_DOWN = moves(lambda y, z, c: (y, (z - 1) % NZ, c))
Y_SWAP = moves(lambda y, z, c: (1 - y, z, c))
C_SWAP = moves(lambda y, z, c: (y, z, 1 - c))


def send(value, step):
    return lax.ppermute(value, "tensor", step)


def sylvester(size):
    i = lax.broadcasted_iota(jnp.int32, (size, size), 0)
    j = lax.broadcasted_iota(jnp.int32, (size, size), 1)
    joined = i & j & 127
    parity = joined
    for shift in (4, 2, 1):
        parity = parity ^ (parity >> shift)
    signs = 1 - 2 * (parity & 1)
    same = (i >> 7) == (j >> 7)
    return jnp.where(same, signs, 0).astype(F32).astype(BF16)


def own_rows(row, y, z, c):
    piece, k, ky, j = row >> 7, (row >> 4) & 7, (row >> 3) & 1, row & 7
    return (((ky ^ y) * NZ + ((k + z) & 7)) * NC + c) * 16 + piece * 8 + j


def attend_kernel(meta, docs, q_own, q_far, e_own, e_far, k_ref, v_ref, a_ref, lim_ref):
    y, z, c = meta[0], meta[1], meta[2]
    rows, tokens = 256, 512
    where = own_rows(lax.broadcasted_iota(jnp.int32, (rows, tokens), 0), y, z, c)
    key = lax.broadcasted_iota(jnp.int32, (rows, tokens), 1)
    seg_q = jnp.zeros((rows, tokens), jnp.int32)
    seg_k = jnp.zeros((rows, tokens), jnp.int32)
    end = jnp.int32(0)
    for i in range(4):
        end = end + docs[i]
        seg_q = seg_q + (where >= end).astype(jnp.int32)
        seg_k = seg_k + (key >= end).astype(jnp.int32)
    allowed = (seg_q == seg_k) & (key <= where)
    pick = (where == key).astype(F32).astype(BF16)
    keys, values = k_ref[...], v_ref[...]
    for side, (q_ref, e_ref) in enumerate(((q_own, e_own), (q_far, e_far))):
        picked = jnp.dot(pick, q_ref[...], preferred_element_type=F32).astype(BF16)
        for head in range(2):
            scores = lax.dot_general(
                picked[:, head * HD : (head + 1) * HD],
                keys,
                (((1,), (1,)), ((), ())),
                preferred_element_type=F32,
            ) * HD ** (-0.5)
            scores = jnp.where(allowed, scores, F32(-1e30))
            top = jnp.max(scores, axis=1, keepdims=True)
            expo = jnp.where(allowed, jnp.exp(scores - top), F32(0.0))
            probs = (expo / jnp.sum(expo, axis=1, keepdims=True)).astype(BF16)
            out = jnp.dot(probs, values, preferred_element_type=F32).astype(BF16)
            at = (side * 2 + head) * HD
            a_ref[:, at : at + HD] = out
        expo_rows = lax.dot_general(
            pick,
            e_ref[...].astype(F32).astype(BF16),
            (((1,), (1,)), ((), ())),
            preferred_element_type=F32,
        )
        limit = jnp.zeros(expo_rows.shape, F32)
        for level in LEVELS:
            limit = limit + jnp.where(expo_rows == level, F32(448.0 * 2.0**level), F32(0.0))
        for tile in range(8):
            lim_ref[tile, side] = limit[:, tile * 8 : tile * 8 + 8]


def attend(meta, docs, q_own, q_far, e_own, e_far, keys, values):
    whole = lambda shape: pl.BlockSpec(shape, lambda i, m, d: (0,) * len(shape))
    head = pl.BlockSpec((512, HD), lambda i, m, d: (0, m[3]))
    return pl.pallas_call(
        attend_kernel,
        out_shape=(
            jax.ShapeDtypeStruct((256, 512), BF16),
            jax.ShapeDtypeStruct((8, 2, 256, 8), F32),
        ),
        grid_spec=pltpu.PrefetchScalarGridSpec(
            num_scalar_prefetch=2,
            grid=(1,),
            in_specs=[
                whole((512, 256)),
                whole((512, 256)),
                whole((64, 512)),
                whole((64, 512)),
                head,
                head,
            ],
            out_specs=(whole((256, 512)), whole((8, 2, 256, 8))),
        ),
        compiler_params=pltpu.CompilerParams(vmem_limit_bytes=32 << 20),
        cost_estimate=pl.CostEstimate(
            flops=400_000_000, bytes_accessed=3_000_000, transcendentals=600_000
        ),
    )(meta, docs, q_own, q_far, e_own, e_far, keys, values)


def project_kernel(a_ref, lim_ref, w_own, w_far, o_ref):
    table = sylvester(256)
    for part in range(4):
        cols = slice(part * 256, part * 256 + 256)
        total = [None, None]
        for side, w_ref in enumerate((w_own, w_far)):
            turned = jnp.dot(w_ref[:, cols], table, preferred_element_type=F32)
            turned = (turned * F32(1.0 / math.sqrt(128.0))).astype(BF16)
            term = jnp.dot(
                a_ref[:, side * 256 : side * 256 + 256], turned, preferred_element_type=F32
            )
            for half in range(2):
                lane = part * 2 + half
                limit = lim_ref[0, side, :, lane : lane + 1]
                kept = jnp.clip(term[:, half * 128 : half * 128 + 128], -limit, limit)
                total[half] = kept if side == 0 else total[half] + kept
        for half in range(2):
            at = part * 256 + half * 128
            o_ref[:, at : at + 128] = total[half].astype(BF16)


def project(attn, limits, w_own, w_far):
    return pl.pallas_call(
        project_kernel,
        out_shape=jax.ShapeDtypeStruct((256, 8192), BF16),
        grid=(8,),
        in_specs=[
            pl.BlockSpec((256, 512), lambda i: (0, 0)),
            pl.BlockSpec((1, 2, 256, 8), lambda i: (i, 0, 0, 0)),
            pl.BlockSpec((256, 1024), lambda i: (0, i)),
            pl.BlockSpec((256, 1024), lambda i: (0, i)),
        ],
        out_specs=pl.BlockSpec((256, 1024), lambda i: (0, i)),
        compiler_params=pltpu.CompilerParams(vmem_limit_bytes=32 << 20),
        cost_estimate=pl.CostEstimate(
            flops=4_300_000_000, bytes_accessed=13_000_000, transcendentals=0
        ),
    )(attn, limits, w_own, w_far)


def norm_kernel(sum_ref, far_ref, res_ref, gain_ref, up_ref, normed_ref):
    total = sum_ref[...].astype(F32) + far_ref[...].astype(F32)
    stacked = jnp.concatenate([total[:, b * 128 : b * 128 + 128] for b in range(64)], axis=0)
    table = sylvester(128)
    high = stacked.astype(BF16)
    rest = stacked - high.astype(F32)
    mid = rest.astype(BF16)
    turned = jnp.dot(high, table, preferred_element_type=F32)
    turned = turned + jnp.dot(mid, table, preferred_element_type=F32)
    turned = turned * F32(1.0 / math.sqrt(128.0))
    mixed = jnp.concatenate([turned[b * 8 : b * 8 + 8] for b in range(64)], axis=1)
    updated = res_ref[...].astype(F32) + mixed
    up_ref[...] = updated.astype(BF16)
    inverse = lax.rsqrt(jnp.mean(updated * updated, axis=1, keepdims=True) + 1e-05)
    normed_ref[...] = (updated * inverse * gain_ref[...].astype(F32)).astype(BF16)


def norm(near, far, residual, gain):
    shape = jax.ShapeDtypeStruct((8, 8192), BF16)
    return pl.pallas_call(
        norm_kernel,
        out_shape=(shape, shape),
        compiler_params=pltpu.CompilerParams(vmem_limit_bytes=16 << 20),
        cost_estimate=pl.CostEstimate(flops=40_000_000, bytes_accessed=600_000, transcendentals=8),
    )(near, far, residual, gain)


def next_kernel(*refs):
    *x_refs, w_ref, o_ref = refs
    total = None
    for at in range(0, 8192, 1024):
        rows = jnp.concatenate([x[:, at : at + 1024] for x in x_refs], axis=0)
        part = jnp.dot(rows, w_ref[at : at + 1024, :], preferred_element_type=F32)
        total = part if total is None else total + part
    o_ref[...] = total.astype(BF16)


def next_rows(chunks, weight):
    count = sum(x.shape[0] for x in chunks)
    return pl.pallas_call(
        next_kernel,
        out_shape=jax.ShapeDtypeStruct((count, 256), BF16),
        compiler_params=pltpu.CompilerParams(vmem_limit_bytes=24 << 20),
        cost_estimate=pl.CostEstimate(
            flops=2 * count * 8192 * 256,
            bytes_accessed=(4 << 20) + count * 16384,
            transcendentals=0,
        ),
    )(*chunks, weight)


def place_kernel(meta, x_ref, o_ref):
    y, z, c = meta[0], meta[1], meta[2]
    to = lax.broadcasted_iota(jnp.int32, (512, 512), 0)
    row = lax.broadcasted_iota(jnp.int32, (512, 512), 1)
    k, kc, piece, ky, j = row >> 6, (row >> 5) & 1, (row >> 4) & 1, (row >> 3) & 1, row & 7
    target = (((ky ^ y) * NZ + ((k + z) & 7)) * NC + (kc ^ c)) * 16 + piece * 8 + j
    pick = (target == to).astype(F32).astype(BF16)
    o_ref[...] = jnp.dot(pick, x_ref[...], preferred_element_type=F32).astype(BF16)


def place(meta, rows):
    return pl.pallas_call(
        place_kernel,
        out_shape=jax.ShapeDtypeStruct((512, 256), BF16),
        grid_spec=pltpu.PrefetchScalarGridSpec(
            num_scalar_prefetch=1,
            grid=(1,),
            in_specs=[pl.BlockSpec((512, 256), lambda i, m: (0, 0))],
            out_specs=pl.BlockSpec((512, 256), lambda i, m: (0, 0)),
        ),
        cost_estimate=pl.CostEstimate(
            flops=140_000_000, bytes_accessed=520_000, transcendentals=0
        ),
    )(meta, rows)


def add(*terms):
    return functools.reduce(lambda a, b: a + b, [t.astype(F32) for t in terms]).astype(BF16)


def reduce_z(terms):
    half = terms[4].shape[1] // 2
    down = send(terms[4][:, :half], Z_DOWN)
    up = send(terms[4][:, half:], Z_UP)
    down = jnp.concatenate([add(terms[5][:, :half], down), terms[5][:, half:]], axis=1)
    up = jnp.concatenate([terms[3][:, :half], add(terms[3][:, half:], up)], axis=1)
    down, up = send(down, Z_DOWN), send(up, Z_UP)
    down, up = send(add(terms[6], down), Z_DOWN), send(add(terms[2], up), Z_UP)
    down, up = send(add(terms[7], down), Z_DOWN), send(add(terms[1], up), Z_UP)
    return add(terms[0], down, up)


def gather_z(own):
    half = own.shape[1] // 2
    got = [own] + [None] * 7
    up = down = own
    for hop in range(1, 4):
        up, down = send(up, Z_UP), send(down, Z_DOWN)
        got[8 - hop], got[hop] = up, down
    got[4] = jnp.concatenate([send(up[:, :half], Z_UP), send(down[:, half:], Z_DOWN)], axis=1)
    return got


def local(
    query, keys, values, out_weight, scale_exp, residual, norm_gain, next_weight, doc_lengths
):
    rank = lax.axis_index("tensor")
    y, z, c = rank // 16, rank // 2 % 8, rank % 2
    meta = jnp.stack([y, z, c, rank // 4]).astype(jnp.int32)
    expo = scale_exp[0].T
    q_far = send(query, C_SWAP)
    e_far = send(expo, C_SWAP)
    w_far = send(out_weight, C_SWAP)
    attn, limits = attend(meta, doc_lengths, query, q_far, expo, e_far, keys, values)
    terms = project(attn, limits, out_weight, w_far)
    gain = norm_gain.reshape(1, -1)
    updated, blocks = [], {}
    for piece in range(2):
        base = piece * 128
        summed = reduce_z([terms[base + k * 16 : base + k * 16 + 16] for k in range(8)])
        far = send(summed[8:], Y_SWAP)
        up, normed = norm(summed[:8], far, residual[piece * 8 : piece * 8 + 8], gain)
        updated.append(up)
        pair = jnp.concatenate([normed, send(normed, Y_SWAP)], axis=0)
        got = gather_z(pair)
        swapped = [send(x, C_SWAP) for x in got]
        for group in ((0, 1, 7), (2, 6), (3, 5), (4,)):
            chunks = [x for k in group for x in (got[k], swapped[k])]
            rows = next_rows(chunks, next_weight)
            for i, k in enumerate(group):
                for kc in range(2):
                    at = (i * 2 + kc) * 16
                    blocks[k, kc, piece] = rows[at : at + 16]
    rows = jnp.concatenate(
        [blocks[k, kc, piece] for k in range(8) for kc in range(2) for piece in range(2)], axis=0
    )
    return place(meta, rows), jnp.concatenate(updated, axis=0)


def solution(mesh):
    return jax.shard_map(
        local,
        mesh=mesh,
        in_specs=(
            P("dp", "tensor"),
            P("dp", None),
            P("dp", None),
            P("tensor", None),
            P("tensor", "dp", None),
            P(("dp", "tensor"), None),
            P(),
            P(None, "tensor"),
            P("dp"),
        ),
        out_specs=(P("dp", "tensor"), P(("dp", "tensor"), None)),
        check_vma=False,
    )
```

```python
import functools
import math

import jax
import jax.numpy as jnp
import numpy as np
from jax import lax
from jax.experimental import pallas as pl
from jax.experimental.pallas import tpu as pltpu
from jax.sharding import PartitionSpec as P

HD = 128
LEVELS = range(-13, -6)
F32 = jnp.float32
BF16 = jnp.bfloat16
D = 8192
HALF = D // 2
TILE = 2048
TILES = D // TILE

NY, NZ, NC = 2, 8, 2


def moves(step):
    def index(y, z, c):
        return (y * NZ + z) * NC + c

    return [
        (index(y, z, c), index(*step(y, z, c)))
        for y in range(NY)
        for z in range(NZ)
        for c in range(NC)
    ]


Z_UP = moves(lambda y, z, c: (y, (z + 1) % NZ, c))
Z_DOWN = moves(lambda y, z, c: (y, (z - 1) % NZ, c))
Y_SWAP = moves(lambda y, z, c: (1 - y, z, c))
C_SWAP = moves(lambda y, z, c: (y, z, 1 - c))


def send(value, step):
    return lax.ppermute(value, "tensor", step)


def row_code(piece, k, ky):
    return [((piece * 8 + k) * 2 + ky) * 8 + j for j in range(8)]


PAIRS = ((5, 3), (6, 2), (7, 1))
ORDER = (5, 3, 6, 2, 7, 1, 0)
CODES = (
    row_code(0, 4, 1)
    + row_code(0, 4, 0)
    + row_code(1, 4, 0)
    + row_code(1, 4, 1)
    + [v for far in (1, 0) for k in ORDER for v in row_code(0, k, far)]
    + [v for k in ORDER for far in (0, 1) for v in row_code(1, k, far)]
)
ROWS = np.array(CODES, np.int32).reshape(256, 1)
SUMS = ((8, D), (8, D), (16, HALF), (16, HALF), (16, D), (16, D), (24, D))
SUMS += ((16, D),) * 3 + ((8, D),) + ((32, D),) * 3 + ((16, D),)


def placed(code, y, z, c):
    j, ky, k, piece = code & 7, (code >> 3) & 1, (code >> 4) & 7, code >> 7
    return (((ky ^ y) * NZ + ((k + z) & 7)) * NC + c) * 16 + piece * 8 + j


def sylvester(size):
    i = lax.broadcasted_iota(jnp.int32, (size, size), 0)
    j = lax.broadcasted_iota(jnp.int32, (size, size), 1)
    joined = i & j & 127
    for shift in (4, 2, 1):
        joined = joined ^ (joined >> shift)
    signs = 1 - 2 * (joined & 1)
    return jnp.where((i >> 7) == (j >> 7), signs, 0).astype(F32).astype(BF16)


def params(limit):
    return pltpu.CompilerParams(vmem_limit_bytes=limit << 20)


def cost(flops, moved, transcendentals=0):
    return pl.CostEstimate(
        flops=flops, bytes_accessed=moved, transcendentals=transcendentals
    )


ANY = pl.BlockSpec(memory_space=pl.ANY)
VMEM = pl.BlockSpec(memory_space=pltpu.VMEM)
TOKEN = jax.ShapeDtypeStruct((8, 128), F32)


def attend_kernel(meta, docs, rows_ref, q_own, q_far, e_own, e_far, k_ref, v_ref, a_ref, l_ref):
    where = placed(rows_ref[...], meta[0], meta[1], meta[2])
    key = lax.broadcasted_iota(jnp.int32, (1, 512), 1)
    seg_q = jnp.zeros((256, 1), jnp.int32)
    seg_k = jnp.zeros((1, 512), jnp.int32)
    end = jnp.int32(0)
    for i in range(4):
        end = end + docs[i]
        seg_q = seg_q + (where >= end).astype(jnp.int32)
        seg_k = seg_k + (key >= end).astype(jnp.int32)
    allowed = (seg_q == seg_k) & (key <= where)
    pick = (where == key).astype(F32).astype(BF16)
    keys, values = k_ref[...], v_ref[...]
    for side, (q_ref, e_ref) in enumerate(((q_own, e_own), (q_far, e_far))):
        picked = jnp.dot(pick, q_ref[...], preferred_element_type=F32).astype(BF16)
        for head in range(2):
            scores = lax.dot_general(
                picked[:, head * HD : (head + 1) * HD],
                keys,
                (((1,), (1,)), ((), ())),
                preferred_element_type=F32,
            ) * HD ** (-0.5)
            scores = jnp.where(allowed, scores, F32(-1e30))
            top = jnp.max(scores, axis=1, keepdims=True)
            expo = jnp.where(allowed, jnp.exp(scores - top), F32(0.0))
            probs = (expo / jnp.sum(expo, axis=1, keepdims=True)).astype(BF16)
            out = jnp.dot(probs, values, preferred_element_type=F32).astype(BF16)
            at = (side * 2 + head) * HD
            a_ref[:, at : at + HD] = out
        level_of = lax.dot_general(
            pick,
            e_ref[...].astype(F32).astype(BF16),
            (((1,), (1,)), ((), ())),
            preferred_element_type=F32,
        )
        limit = jnp.zeros(level_of.shape, F32)
        for level in LEVELS:
            bound = F32(448.0 * math.sqrt(128.0) * 2.0**level)
            limit = limit + jnp.where(level_of == level, bound, F32(0.0))
        l_ref[side] = limit


def attend(meta, docs, q_own, q_far, e_own, e_far, keys, values):
    def whole(*shape):
        return pl.BlockSpec(shape, lambda i, m, d: (0,) * len(shape))

    head = pl.BlockSpec((512, HD), lambda i, m, d: (0, m[3]))
    q_block, e_block = whole(512, 256), whole(64, 512)
    return pl.pallas_call(
        attend_kernel,
        out_shape=(
            jax.ShapeDtypeStruct((256, 512), BF16),
            jax.ShapeDtypeStruct((2, 256, 64), F32),
        ),
        grid_spec=pltpu.PrefetchScalarGridSpec(
            num_scalar_prefetch=2,
            grid=(1,),
            in_specs=[whole(256, 1), q_block, q_block, e_block, e_block, head, head],
            out_specs=(whole(256, 512), whole(2, 256, 64)),
        ),
        compiler_params=params(56),
        cost_estimate=cost(400_000_000, 2_000_000, 600_000),
    )(meta, docs, jnp.asarray(ROWS), q_own, q_far, e_own, e_far, keys, values)


def turn_kernel(w_ref, o_ref):
    table = sylvester(256)
    for at in range(0, TILE, 256):
        turned = jnp.dot(w_ref[:, at : at + 256], table, preferred_element_type=F32)
        o_ref[:, at : at + 256] = turned.astype(BF16)


def turn(weight):
    block = pl.BlockSpec((256, TILE), lambda i: (0, i))
    return pl.pallas_call(
        turn_kernel,
        out_shape=jax.ShapeDtypeStruct((256, D), BF16),
        grid=(TILES,),
        in_specs=[block],
        out_specs=block,
        compiler_params=params(56),
        cost_estimate=cost(1_000_000_000, 8 << 20),
    )(weight)


def project_kernel(a_ref, l_ref, w_own, w_far, *refs):
    *outs, turned, bounds = refs
    tile = pl.program_id(0)
    wide = TILE // 128

    @pl.when(tile == 0)
    def _():
        for side in range(2):
            for i in range(TILES):
                bounds[i, side] = l_ref[side, :, i * wide : (i + 1) * wide]

    table = sylvester(256)
    for at in range(0, TILE, 256):
        value = jnp.dot(w_far[:, at : at + 256], table, preferred_element_type=F32)
        turned[:, at : at + 256] = value.astype(BF16)
    for at in range(0, TILE, 256):
        terms = []
        for side, w_ref in enumerate((w_own, turned)):
            term = jnp.dot(
                a_ref[:, side * 256 : side * 256 + 256],
                w_ref[:, at : at + 256],
                preferred_element_type=F32,
            )
            for half in range(2):
                lane = at // 128 + half
                limit = jnp.broadcast_to(bounds[tile, side, :, lane : lane + 1], (256, 128))
                kept = term[:, half * 128 : half * 128 + 128]
                terms.append(jnp.maximum(jnp.minimum(kept, limit), -limit))
        total = jnp.concatenate([terms[0] + terms[2], terms[1] + terms[3]], axis=1)
        cols = slice(at, at + 256)
        row = 0
        for i, o_ref in enumerate(outs):
            count = o_ref.shape[0]
            if i == 3:
                row -= count
            part = total[row : row + count].astype(BF16)
            row += count
            if i in (2, 3):

                @pl.when((tile < TILES // 2) if i == 2 else (tile >= TILES // 2))
                def _():
                    o_ref[:, cols] = part

            else:
                o_ref[:, cols] = part


def project(attn, limits, w_own, w_far):
    last = TILES // 2 - 1
    plain = lambda i: (0, i)
    maps = [plain] * len(SUMS)
    maps[2] = lambda i: (0, jnp.minimum(i, last))
    maps[3] = lambda i: (0, jnp.maximum(i - last - 1, 0))
    w_block = pl.BlockSpec((256, TILE), plain)
    return pl.pallas_call(
        project_kernel,
        out_shape=tuple(jax.ShapeDtypeStruct(s, BF16) for s in SUMS),
        grid=(TILES,),
        in_specs=[
            pl.BlockSpec((256, 512), lambda i: (0, 0)),
            pl.BlockSpec((2, 256, 64), lambda i: (0, 0, 0)),
            w_block,
            w_block,
        ],
        out_specs=tuple(pl.BlockSpec((s[0], TILE), m) for s, m in zip(SUMS, maps)),
        scratch_shapes=[
            pltpu.VMEM((256, TILE), BF16),
            pltpu.VMEM((TILES, 2, 256, TILE // 128), F32),
        ],
        compiler_params=params(58),
        cost_estimate=cost(4_300_000_000, 13_000_000),
    )(attn, limits, w_own, w_far)


def step_kernel(body, n_in, *refs):
    ins, outs, token = refs[:n_in], refs[n_in + 1 : -1], refs[-1]
    values = body(*[r[...].astype(F32) for r in ins])
    for o_ref, value in zip(outs, values):
        o_ref[...] = value.astype(o_ref.dtype)
    token[...] = jnp.zeros((8, 128), F32)


def stage(body, ins, outs, token, span=15):
    *results, token = pl.pallas_call(
        functools.partial(step_kernel, body, len(ins)),
        out_shape=tuple(jax.ShapeDtypeStruct(s, BF16) for s in outs) + (TOKEN,),
        in_specs=[VMEM] * len(ins) + [ANY],
        out_specs=(VMEM,) * (len(outs) + 1),
        compiler_params=params(24),
        cost_estimate=cost(span * 1_150_000_000, span * 3_600_000),
    )(*ins, token)
    return results, token


def finish(total, residual, gain):
    stacked = jnp.concatenate([total[:, b * 128 : b * 128 + 128] for b in range(64)], axis=0)
    table = sylvester(128)
    high = stacked.astype(BF16)
    low = (stacked - high.astype(F32)).astype(BF16)
    turned = jnp.dot(high, table, preferred_element_type=F32)
    turned = turned + jnp.dot(low, table, preferred_element_type=F32)
    turned = turned * F32(1.0 / 128.0)
    mixed = jnp.concatenate([turned[b * 8 : b * 8 + 8] for b in range(64)], axis=1)
    updated = residual + mixed
    inverse = lax.rsqrt(jnp.mean(updated * updated, axis=1, keepdims=True) + 1e-05)
    return updated * inverse * gain, updated


def halves(both, half_down, half_up):
    rows = half_down.shape[0]
    down, up = both[:rows], both[rows:]
    down = jnp.concatenate([down[:, :HALF] + half_down, down[:, HALF:]], axis=1)
    up = jnp.concatenate([up[:, :HALF], up[:, HALF:] + half_up], axis=1)
    return down, up


def next_kernel(*refs):
    *x_refs, w_ref, _, o_ref, token = refs
    token[...] = jnp.zeros((8, 128), F32)
    total = None
    for at in range(0, D, 1024):
        rows = jnp.concatenate([x[:, at : at + 1024].astype(F32) for x in x_refs], axis=0)
        part = jnp.dot(
            rows.astype(BF16), w_ref[at : at + 1024, :], preferred_element_type=F32
        )
        total = part if total is None else total + part
    o_ref[...] = total.astype(BF16)


def next_rows(chunks, weight, token):
    count = sum(x.shape[0] for x in chunks)
    return pl.pallas_call(
        next_kernel,
        out_shape=(jax.ShapeDtypeStruct((count, 256), BF16), TOKEN),
        in_specs=[VMEM] * (len(chunks) + 1) + [ANY],
        out_specs=(VMEM, VMEM),
        compiler_params=params(24),
        cost_estimate=cost(2 * count * D * 256, (4 << 20) + count * 16384),
    )(*chunks, weight, token)


def place_kernel(meta, code_ref, *refs):
    *x_refs, o_ref = refs
    code = code_ref[...]
    target = placed(code & 255, meta[0], meta[1], (code >> 8) ^ meta[2])
    to = lax.broadcasted_iota(jnp.int32, (512, 512), 0)
    pick = (target == to).astype(F32).astype(BF16)
    rows = jnp.concatenate([x[...] for x in x_refs], axis=0)
    o_ref[...] = jnp.dot(pick, rows, preferred_element_type=F32).astype(BF16)


def place(meta, codes, groups):
    table = np.array(codes, np.int32).reshape(1, 512)
    return pl.pallas_call(
        place_kernel,
        out_shape=jax.ShapeDtypeStruct((512, 256), BF16),
        grid_spec=pltpu.PrefetchScalarGridSpec(
            num_scalar_prefetch=1,
            grid=(1,),
            in_specs=[
                pl.BlockSpec(x.shape, lambda i, m: (0, 0)) for x in (table, *groups)
            ],
            out_specs=pl.BlockSpec((512, 256), lambda i, m: (0, 0)),
        ),
        compiler_params=params(16),
        cost_estimate=cost(140_000_000, 520_000),
    )(meta, jnp.asarray(table), *groups)


def local(
    query, keys, values, out_weight, scale_exp, residual, norm_gain, next_weight, doc_lengths
):
    rank = lax.axis_index("tensor")
    meta = jnp.stack([rank >> 4, (rank >> 1) & 7, rank & 1, rank >> 2]).astype(jnp.int32)
    expo = scale_exp[0].T
    q_far = send(query, C_SWAP)
    e_far = send(expo, C_SWAP)
    held_weight, meta = lax.optimization_barrier((out_weight, meta))
    w_far = send(held_weight, C_SWAP)
    attn, limits = attend(meta, doc_lengths, query, q_far, expo, e_far, keys, values)
    sums = project(attn, limits, turn(out_weight), w_far)
    p_send, p_own, q_down, q_up = sums[:4]
    p_sends, p_owns, q_owns = sums[4:7], sums[7:11], sums[11:15]
    gain = norm_gain.reshape(1, -1)

    token = jnp.zeros((8, 128), F32)
    q_down, q_up = send(q_down, Z_DOWN), send(q_up, Z_UP)
    p_got = send(p_send, Y_SWAP)
    p_gots = [send(x, Y_SWAP) for x in p_sends]
    (p_down, p_up), token = stage(
        lambda a, b: ((a + b)[:, :HALF], (a + b)[:, HALF:]),
        (p_own, p_got),
        ((8, HALF), (8, HALF)),
        token,
    )
    p_down, p_up = send(p_down, Z_DOWN), send(p_up, Z_UP)
    for step in range(3):
        if step == 0:
            q_body = halves
            p_body = lambda a, b, d, u: halves(a + b, d, u)
        else:
            q_body = lambda a, d, u: (a[:16] + d, a[16:] + u)
            p_body = lambda a, b, d, u: (a[:8] + b[:8] + d, a[8:] + b[8:16] + u)
        (q_down, q_up), token = stage(
            q_body, (q_owns[step], q_down, q_up), ((16, D), (16, D)), token
        )
        q_down, q_up = send(q_down, Z_DOWN), send(q_up, Z_UP)
        (p_down, p_up), token = stage(
            p_body, (p_owns[step], p_gots[step], p_down, p_up), ((8, D), (8, D)), token
        )
        p_down, p_up = send(p_down, Z_DOWN), send(p_up, Z_UP)
    (q_near, q_send), token = stage(
        lambda a, d, u: ((a + d + u)[:8], (a + d + u)[8:]),
        (q_owns[3], q_down, q_up),
        ((8, D), (8, D)),
        token,
    )
    q_got = send(q_send, Y_SWAP)
    (p_norm, p_updated), token = stage(
        lambda a, b, d, u, r, g: finish(a + b[16:] + d + u, r, g),
        (p_owns[3], p_gots[2], p_down, p_up, residual[:8], gain),
        ((8, D), (8, D)),
        token,
    )
    (q_norm, q_updated), token = stage(
        lambda a, b, r, g: finish(a + b, r, g),
        (q_near, q_got, residual[8:], gain),
        ((8, D), (8, D)),
        token,
    )

    groups, codes = [], []

    def multiply(chunks, token):
        rows, token = next_rows([x for x, _ in chunks], next_weight, token)
        groups.append(rows)
        for _, code in chunks:
            codes.extend(code)
        return token

    def cores(value, code):
        return [(value, code), (send(value, C_SWAP), [256 + v for v in code])]

    def rows(piece, far, *chips):
        return [v for k in chips for ky in far for v in row_code(piece, k, ky)]

    def stack(*parts):
        return jnp.concatenate(parts, axis=0)

    p_up, p_down = send(p_norm, Z_UP), send(p_norm, Z_DOWN)
    q_far = send(q_norm, Y_SWAP)
    (q_pair,), token = stage(lambda a, b: (stack(a, b),), (q_norm, q_far), ((16, D),), token)
    q_up, q_down = send(q_pair, Z_UP), send(q_pair, Z_DOWN)
    p_held, p_held_chips = (p_norm,), (0,)
    q_held, q_held_code = (q_pair,), rows(1, (0, 1), 0)
    ready = None
    for hop in range(1, 4):
        chips = (8 - hop, hop)
        count = 8 * len(p_held) + 16
        (p_up, p_down, p_both), token = stage(
            lambda u, d, *h: (u, d, stack(*h, u, d)),
            (p_up, p_down, *p_held),
            ((8, D), (8, D), (count, D)),
            token,
        )
        p_chips = p_held_chips + chips
        if hop < 3:
            p_up, p_down = send(p_up, Z_UP), send(p_down, Z_DOWN)
        else:
            p_up, p_down = send(p_up[:, :HALF], Z_UP), send(p_down[:, HALF:], Z_DOWN)
        p_far = send(p_both, Y_SWAP)
        if ready is not None:
            token = multiply(ready, token)
        whole = (p_both, *q_held)
        (q_up, q_down, packed), token = stage(
            lambda u, d, *h: (u, d, stack(*h, u, d)),
            (q_up, q_down, *whole),
            ((16, D), (16, D), (32 + sum(x.shape[0] for x in whole), D)),
            token,
        )
        code = rows(0, (0,), *p_chips) + q_held_code + rows(1, (0, 1), *chips)
        if hop < 3:
            q_up, q_down = send(q_up, Z_UP), send(q_down, Z_DOWN)
        else:
            q_up, q_down = send(q_up[:, :HALF], Z_UP), send(q_down[:, HALF:], Z_DOWN)
        ready = cores(packed, code)
        q_held, q_held_code = (p_far,), rows(0, (1,), *p_chips)
        p_held, p_held_chips = (), ()
    (p_last,), token = stage(
        lambda u, d: (jnp.concatenate([u, d], axis=1),), (p_up, p_down), ((8, D),), token
    )
    p_far = send(p_last, Y_SWAP)
    token = multiply(ready, token)
    (packed,), token = stage(
        lambda u, d, *h: (stack(*h, jnp.concatenate([u, d], axis=1)),),
        (q_up, q_down, p_last, *q_held),
        ((40, D),),
        token,
        1,
    )
    last = cores(packed, rows(0, (0,), 4) + q_held_code + rows(1, (0, 1), 4))
    last += cores(p_far, rows(0, (1,), 4))
    multiply(last, token)
    return place(meta, codes, groups), jnp.concatenate([p_updated, q_updated], axis=0)


def solution(mesh):
    return jax.shard_map(
        local,
        mesh=mesh,
        in_specs=(
            P("dp", "tensor"),
            P("dp", None),
            P("dp", None),
            P("tensor", None),
            P("tensor", "dp", None),
            P(("dp", "tensor"), None),
            P(),
            P(None, "tensor"),
            P("dp"),
        ),
        out_specs=(P("dp", "tensor"), P(("dp", "tensor"), None)),
        check_vma=False,
    )
```

```python
import functools
import math

import jax
import jax.numpy as jnp
import numpy as np
from jax import lax
from jax.experimental import pallas as pl
from jax.experimental.pallas import tpu as pltpu
from jax.sharding import PartitionSpec as P

HD = 128
LEVELS = range(-13, -6)
F32 = jnp.float32
BF16 = jnp.bfloat16
D = 8192
HALF = D // 2
TILE = 2048
TILES = D // TILE

NY, NZ, NC = 2, 8, 2


def moves(step):
    def index(y, z, c):
        return (y * NZ + z) * NC + c

    return [
        (index(y, z, c), index(*step(y, z, c)))
        for y in range(NY)
        for z in range(NZ)
        for c in range(NC)
    ]


Z_UP = moves(lambda y, z, c: (y, (z + 1) % NZ, c))
Z_DOWN = moves(lambda y, z, c: (y, (z - 1) % NZ, c))
Y_SWAP = moves(lambda y, z, c: (1 - y, z, c))
C_SWAP = moves(lambda y, z, c: (y, z, 1 - c))


def send(value, step):
    return lax.ppermute(value, "tensor", step)


def row_code(piece, k, ky):
    return [((piece * 8 + k) * 2 + ky) * 8 + j for j in range(8)]


PAIRS = ((5, 3), (6, 2), (7, 1))
ORDER = (5, 3, 6, 2, 7, 1, 0)
CODES = (
    [v for k in (4, *ORDER) for v in row_code(0, k, 1)]
    + row_code(0, 4, 0)
    + row_code(1, 4, 0)
    + row_code(1, 4, 1)
    + [v for k in ORDER for v in row_code(0, k, 0)]
    + [v for k in ORDER for far in (0, 1) for v in row_code(1, k, far)]
)
ROWS = np.array(CODES, np.int32).reshape(1, 256)
SUMS = (24, 40, 8, 16, 16, 16, 16, 8, 32, 32, 32, 16)
SPLIT = 3


def placed(code, y, z, c):
    j, ky, k, piece = code & 7, (code >> 3) & 1, (code >> 4) & 7, code >> 7
    return (((ky ^ y) * NZ + ((k + z) & 7)) * NC + c) * 16 + piece * 8 + j


def sylvester(size):
    i = lax.broadcasted_iota(jnp.int32, (size, size), 0)
    j = lax.broadcasted_iota(jnp.int32, (size, size), 1)
    joined = i & j & 127
    for shift in (4, 2, 1):
        joined = joined ^ (joined >> shift)
    signs = 1 - 2 * (joined & 1)
    return jnp.where((i >> 7) == (j >> 7), signs, 0).astype(F32).astype(BF16)


def params(limit):
    return pltpu.CompilerParams(vmem_limit_bytes=limit << 20)


def cost(flops, moved, transcendentals=0):
    return pl.CostEstimate(
        flops=flops, bytes_accessed=moved, transcendentals=transcendentals
    )


ANY = pl.BlockSpec(memory_space=pl.ANY)
VMEM = pl.BlockSpec(memory_space=pltpu.VMEM)
TOKEN = jax.ShapeDtypeStruct((8, 128), F32)


A_COLS = 384


def attend_kernel(meta, docs, rows_ref, q_ref, e_ref, k_ref, v_ref, near_ref, far_ref):
    key = lax.broadcasted_iota(jnp.int32, (1, 512), 1)
    at = pl.ds(pl.multiple_of(meta[3] * HD, HD), HD)
    keys, values = k_ref[:, at], v_ref[:, at]
    seg_k = jnp.zeros((1, 512), jnp.int32)
    end = jnp.int32(0)
    for i in range(4):
        end = end + docs[i]
        seg_k = seg_k + (key >= end).astype(jnp.int32)
    levels = e_ref[...].astype(F32).astype(BF16)
    codes = jnp.broadcast_to(rows_ref[...], (8, 256)).T[:, :1]
    for side, o_ref in ((1, far_ref), (0, near_ref)):
        where = placed(codes, meta[0], meta[1], meta[2] ^ side)
        seg_q = jnp.zeros((256, 1), jnp.int32)
        end = jnp.int32(0)
        for i in range(4):
            end = end + docs[i]
            seg_q = seg_q + (where >= end).astype(jnp.int32)
        allowed = (seg_q == seg_k) & (key <= where)
        pick = (where == key).astype(F32).astype(BF16)
        picked = jnp.dot(pick, q_ref[...], preferred_element_type=F32).astype(BF16)
        for head in range(2):
            scores = lax.dot_general(
                picked[:, head * HD : (head + 1) * HD],
                keys,
                (((1,), (1,)), ((), ())),
                preferred_element_type=F32,
            ) * HD ** (-0.5)
            scores = jnp.where(allowed, scores, F32(-1e30))
            top = jnp.max(scores, axis=1, keepdims=True)
            expo = jnp.where(allowed, jnp.exp(scores - top), F32(0.0))
            probs = (expo / jnp.sum(expo, axis=1, keepdims=True)).astype(BF16)
            out = jnp.dot(probs, values, preferred_element_type=F32).astype(BF16)
            o_ref[:, head * HD : (head + 1) * HD] = out
        level_of = lax.dot_general(
            pick, levels, (((1,), (1,)), ((), ())), preferred_element_type=F32
        )
        limit = jnp.zeros(level_of.shape, F32)
        for level in LEVELS:
            limit = limit + jnp.where(level_of == level, F32(448.0 * 2.0**level), F32(0.0))
        limit = jnp.concatenate([limit, jnp.zeros((256, 64), F32)], axis=1)
        o_ref[:, 256:] = limit.astype(BF16)


def attend(meta, docs, query, expo, keys, values):
    scalars = pl.BlockSpec(memory_space=pltpu.SMEM)
    shape = jax.ShapeDtypeStruct((256, A_COLS), BF16)
    return pl.pallas_call(
        attend_kernel,
        out_shape=(shape, shape),
        in_specs=[scalars, scalars] + [VMEM] * 5,
        out_specs=(VMEM, VMEM),
        compiler_params=params(16),
        cost_estimate=cost(6_000_000_000, 2_000_000, 600_000),
    )(meta, docs, jnp.asarray(ROWS), query, expo, keys, values)


CHUNK = 64


def turn_kernel(w_ref, left_ref, right_ref, buffer, result, in_sems, out_sems):
    parts = 256 // CHUNK
    copies, stores = [], []
    for i in range(parts):
        rows = pl.ds(i * CHUNK, CHUNK)
        copies.append(pltpu.make_async_copy(w_ref.at[rows], buffer.at[i], in_sems.at[i]))
        copies[i].start()
    table = sylvester(256)
    for i in range(parts):
        copies[i].wait()
        for half, o_ref in enumerate((left_ref, right_ref)):
            starts = range(half * HALF, (half + 1) * HALF, 256)
            blocks = jnp.concatenate([buffer[i, :, at : at + 256] for at in starts], axis=0)
            turned = jnp.dot(blocks, table, preferred_element_type=F32).astype(BF16)
            for n in range(HALF // 256):
                result[i, half, :, n * 256 : n * 256 + 256] = turned[
                    n * CHUNK : (n + 1) * CHUNK
                ]
            rows = pl.ds(i * CHUNK, CHUNK)
            stores.append(
                pltpu.make_async_copy(
                    result.at[i, half], o_ref.at[rows], out_sems.at[i, half]
                )
            )
            stores[-1].start()
    for store in stores:
        store.wait()


def turn(weight):
    parts = 256 // CHUNK
    shape = jax.ShapeDtypeStruct((256, HALF), BF16)
    hbm = pl.BlockSpec(memory_space=pltpu.HBM)
    return pl.pallas_call(
        turn_kernel,
        out_shape=(shape, shape),
        in_specs=[hbm],
        out_specs=(hbm, hbm),
        scratch_shapes=[
            pltpu.VMEM((parts, CHUNK, D), BF16),
            pltpu.VMEM((parts, 2, CHUNK, HALF), BF16),
            pltpu.SemaphoreType.DMA((parts,)),
            pltpu.SemaphoreType.DMA((parts, 2)),
        ],
        compiler_params=params(61),
        cost_estimate=cost(4_000_000_000, 8 << 20),
    )(weight)


def project_kernel(half, a_own, a_far, w_own, w_far, *refs):
    outs, bounds = refs[-1 - len(SUMS) : -1], refs[-1]
    tile = pl.program_id(0)
    wide = TILE // 128
    count = HALF // TILE

    @pl.when(tile == 0)
    def _():
        for side, a_ref in enumerate((a_own, a_far)):
            limits = a_ref[:, 256:].astype(F32) * F32(math.sqrt(128.0))
            for i in range(count):
                at = (half * count + i) * wide
                bounds[i, side] = limits[:, at : at + wide]

    for at in range(0, TILE, 256):
        terms = []
        for side, (a_ref, w_ref) in enumerate(((a_own, w_own), (a_far, w_far))):
            term = jnp.dot(
                a_ref[:, :256],
                w_ref[:, at : at + 256],
                preferred_element_type=F32,
            )
            for part in range(2):
                lane = at // 128 + part
                limit = jnp.broadcast_to(bounds[tile, side, :, lane : lane + 1], (256, 128))
                kept = term[:, part * 128 : part * 128 + 128]
                terms.append(jnp.maximum(jnp.minimum(kept, limit), -limit))
        total = jnp.concatenate([terms[0] + terms[2], terms[1] + terms[3]], axis=1)
        row = 0
        for o_ref in outs:
            count_rows = o_ref.shape[0]
            o_ref[:, at : at + 256] = total[row : row + count_rows].astype(BF16)
            row += count_rows


def project(half, a_own, a_far, w_own, w_far, sums=None):
    first = half * (HALF // TILE)
    here = pl.BlockSpec((256, TILE), lambda i: (0, i))
    shapes = [(count, HALF if at == SPLIT else D) for at, count in enumerate(SUMS)]
    maps = [
        (lambda i: (0, i)) if at == SPLIT else (lambda i: (0, i + first))
        for at in range(len(SUMS))
    ]
    given = [] if sums is None else [x for at, x in enumerate(sums) if at != SPLIT]
    into = [at for at in range(len(SUMS)) if at != SPLIT]
    return pl.pallas_call(
        functools.partial(project_kernel, half),
        out_shape=tuple(jax.ShapeDtypeStruct(s, BF16) for s in shapes),
        grid=(HALF // TILE,),
        in_specs=[
            pl.BlockSpec((256, A_COLS), lambda i: (0, 0)),
            pl.BlockSpec((256, A_COLS), lambda i: (0, 0)),
            here,
            here,
        ]
        + [ANY] * len(given),
        out_specs=tuple(pl.BlockSpec((s[0], TILE), m) for s, m in zip(shapes, maps)),
        scratch_shapes=[pltpu.VMEM((HALF // TILE, 2, 256, TILE // 128), F32)],
        input_output_aliases={4 + i: into[i] for i in range(len(given))},
        compiler_params=params(24),
        cost_estimate=cost(4_000_000_000, 6_500_000),
    )(a_own, a_far, w_own, w_far, *given)


def step_kernel(body, n_in, *refs):
    ins, outs, token = refs[:n_in], refs[n_in + 1 : -1], refs[-1]
    values = body(*[r[...].astype(F32) for r in ins])
    for o_ref, value in zip(outs, values):
        o_ref[...] = value.astype(o_ref.dtype)
    token[...] = jnp.zeros((8, 128), F32)


def stage(body, ins, outs, token, span=15):
    *results, token = pl.pallas_call(
        functools.partial(step_kernel, body, len(ins)),
        out_shape=tuple(jax.ShapeDtypeStruct(s, BF16) for s in outs) + (TOKEN,),
        in_specs=[VMEM] * len(ins) + [ANY],
        out_specs=(VMEM,) * (len(outs) + 1),
        compiler_params=params(24),
        cost_estimate=cost(span * 1_150_000_000, span * 3_600_000),
    )(*ins, token)
    return results, token


def finish(total, residual, gain):
    stacked = jnp.concatenate([total[:, b * 128 : b * 128 + 128] for b in range(64)], axis=0)
    table = sylvester(128)
    high = stacked.astype(BF16)
    low = (stacked - high.astype(F32)).astype(BF16)
    turned = jnp.dot(high, table, preferred_element_type=F32)
    turned = turned + jnp.dot(low, table, preferred_element_type=F32)
    turned = turned * F32(1.0 / 128.0)
    mixed = jnp.concatenate([turned[b * 8 : b * 8 + 8] for b in range(64)], axis=1)
    updated = residual + mixed
    inverse = lax.rsqrt(jnp.mean(updated * updated, axis=1, keepdims=True) + 1e-05)
    return updated * inverse * gain, updated


def halves(both, half_down, half_up):
    rows = half_down.shape[0]
    down, up = both[:rows], both[rows:]
    down = jnp.concatenate([down[:, :HALF] + half_down, down[:, HALF:]], axis=1)
    up = jnp.concatenate([up[:, :HALF], up[:, HALF:] + half_up], axis=1)
    return down, up


def times(x_refs, w_ref):
    total = None
    for at in range(0, D, 1024):
        rows = jnp.concatenate([x[:, at : at + 1024].astype(F32) for x in x_refs], axis=0)
        part = jnp.dot(
            rows.astype(BF16), w_ref[at : at + 1024, :], preferred_element_type=F32
        )
        total = part if total is None else total + part
    return total


def next_kernel(*refs):
    *x_refs, w_ref, _, o_ref, token = refs
    token[...] = jnp.zeros((8, 128), F32)
    o_ref[...] = times(x_refs, w_ref).astype(BF16)


def next_rows(chunks, weight, token):
    count = sum(x.shape[0] for x in chunks)
    return pl.pallas_call(
        next_kernel,
        out_shape=(jax.ShapeDtypeStruct((count, 256), BF16), TOKEN),
        in_specs=[VMEM] * (len(chunks) + 1) + [ANY],
        out_specs=(VMEM, VMEM),
        compiler_params=params(24),
        cost_estimate=cost(2 * count * D * 256, (4 << 20) + count * 16384),
    )(*chunks, weight, token)


def last_kernel(n_rows, n_groups, meta, code_ref, *refs):
    groups, x_refs = refs[:n_groups], refs[n_groups : n_groups + 1]
    w_ref, o_ref = refs[n_groups + 1], refs[-1]
    code = code_ref[...]
    target = placed(code & 255, meta[0], meta[1], (code >> 8) ^ meta[2])
    to = lax.broadcasted_iota(jnp.int32, (512, n_rows), 0)
    pick = (target == to).astype(F32).astype(BF16)
    rows = [x[...] for x in groups] + [times(x_refs, w_ref).astype(BF16)]
    rows = jnp.concatenate([x.astype(F32) for x in rows], axis=0).astype(BF16)
    value = jnp.dot(pick, rows, preferred_element_type=F32)
    if len(refs) > n_groups + 3:
        value = value + refs[n_groups + 2][...]
    o_ref[...] = value.astype(o_ref.dtype)


def last_rows(meta, codes, groups, chunk, weight, *sofar):
    table = np.array(codes, np.int32).reshape(1, -1)
    count = table.shape[1]
    return pl.pallas_call(
        functools.partial(last_kernel, count, len(groups)),
        out_shape=jax.ShapeDtypeStruct((512, 256), BF16 if sofar else F32),
        in_specs=[pl.BlockSpec(memory_space=pltpu.SMEM)]
        + [VMEM] * (len(groups) + 3 + len(sofar)),
        out_specs=VMEM,
        compiler_params=params(24),
        cost_estimate=cost(1_000_000_000, 6 << 20),
    )(meta, jnp.asarray(table), *groups, chunk, weight, *sofar)


def local(
    query, keys, values, out_weight, scale_exp, residual, norm_gain, next_weight, doc_lengths
):
    rank = lax.axis_index("tensor")
    meta = jnp.stack([rank >> 4, (rank >> 1) & 7, rank & 1, rank >> 2]).astype(jnp.int32)
    expo = scale_exp[0].T
    w_own = turn(out_weight)
    w_far = [send(w, C_SWAP) for w in w_own]
    a_own, a_send = attend(meta, doc_lengths, query, expo, keys, values)
    a_far = send(a_send, C_SWAP)
    sums = project(0, a_own, a_far, w_own[0], w_far[0])
    q_down = sums[SPLIT]
    sums = project(1, a_own, a_far, w_own[1], w_far[1], sums)
    p_send, p_later, p_own, q_up = sums[:4]
    p_owns, q_owns = sums[4:8], sums[8:12]
    gain = norm_gain.reshape(1, -1)

    token = jnp.zeros((8, 128), F32)
    q_down, q_up = send(q_down, Z_DOWN), send(q_up, Z_UP)
    p_got, p_rest = send(p_send, Y_SWAP), send(p_later, Y_SWAP)
    for step in range(4):
        if step < 3:
            q_body = halves if step == 0 else lambda a, d, u: (a[:16] + d, a[16:] + u)
            (q_down, q_up), token = stage(
                q_body, (q_owns[step], q_down, q_up), ((16, D), (16, D)), token
            )
            q_down, q_up = send(q_down, Z_DOWN), send(q_up, Z_UP)
        else:
            (q_near, q_send), token = stage(
                lambda a, d, u: ((a + d + u)[:8], (a + d + u)[8:]),
                (q_owns[3], q_down, q_up),
                ((8, D), (8, D)),
                token,
            )
        if step == 0:
            (p_down, p_up), token = stage(
                lambda a, b: ((a + b[:8])[:, :HALF], (a + b[:8])[:, HALF:]),
                (p_own, p_got),
                ((8, HALF), (8, HALF)),
                token,
            )
        else:
            at = step * 16 - 32
            if step == 1:
                p_body = lambda a, b, d, u: halves(a + b[8:], d, u)
            else:
                p_body = lambda a, b, d, u, at=at: (
                    a[:8] + b[at : at + 8] + d,
                    a[8:] + b[at + 8 : at + 16] + u,
                )
            (p_down, p_up), token = stage(
                p_body,
                (p_owns[step - 1], p_got if step == 1 else p_rest, p_down, p_up),
                ((8, D), (8, D)),
                token,
            )
        p_down, p_up = send(p_down, Z_DOWN), send(p_up, Z_UP)
    q_got = send(q_send, Y_SWAP)
    (q_norm, q_updated), token = stage(
        lambda a, b, r, g: finish(a + b, r, g),
        (q_near, q_got, residual[8:], gain),
        ((8, D), (8, D)),
        token,
    )
    (p_norm, p_updated), token = stage(
        lambda a, b, d, u, r, g: finish(a + b[32:] + d + u, r, g),
        (p_owns[3], p_rest, p_down, p_up, residual[:8], gain),
        ((8, D), (8, D)),
        token,
    )

    groups, codes = [], []

    def multiply(chunks, token):
        rows, token = next_rows([x for x, _ in chunks], next_weight, token)
        groups.append(rows)
        for _, code in chunks:
            codes.extend(code)
        return token

    def cores(value, code):
        return [(value, code), (send(value, C_SWAP), [256 + v for v in code])]

    def rows(piece, far, *chips):
        return [v for k in chips for ky in far for v in row_code(piece, k, ky)]

    def stack(*parts):
        return jnp.concatenate(parts, axis=0)

    p_up, p_down = send(p_norm, Z_UP), send(p_norm, Z_DOWN)
    q_far = send(q_norm, Y_SWAP)
    (q_pair,), token = stage(lambda a, b: (stack(a, b),), (q_norm, q_far), ((16, D),), token, 1)
    q_up, q_down = send(q_pair, Z_UP), send(q_pair, Z_DOWN)
    p_held, p_held_chips = (p_norm,), (0,)
    q_held, q_held_code = (q_pair,), rows(1, (0, 1), 0)
    ready = None
    for hop in range(1, 4):
        chips = (8 - hop, hop)
        count = 8 * len(p_held) + 16
        (p_up, p_down, p_both), token = stage(
            lambda u, d, *h: (u, d, stack(*h, u, d)),
            (p_up, p_down, *p_held),
            ((8, D), (8, D), (count, D)),
            token,
        )
        if hop == 1:
            (updated,), token = stage(
                lambda a, b: (stack(a, b),), (p_updated, q_updated), ((16, D),), token, 1
            )
        p_chips = p_held_chips + chips
        if hop < 3:
            p_up, p_down = send(p_up, Z_UP), send(p_down, Z_DOWN)
        else:
            p_up, p_down = send(p_up[:, :HALF], Z_UP), send(p_down[:, HALF:], Z_DOWN)
        p_far = send(p_both, Y_SWAP)
        if ready is not None:
            token = multiply(ready, token)
        whole = (p_both, *q_held)
        (q_up, q_down, packed), token = stage(
            lambda u, d, *h: (u, d, stack(*h, u, d)),
            (q_up, q_down, *whole),
            ((16, D), (16, D), (32 + sum(x.shape[0] for x in whole), D)),
            token,
        )
        code = rows(0, (0,), *p_chips) + q_held_code + rows(1, (0, 1), *chips)
        if hop < 3:
            q_up, q_down = send(q_up, Z_UP), send(q_down, Z_DOWN)
        else:
            q_up, q_down = send(q_up[:, :HALF], Z_UP), send(q_down[:, HALF:], Z_DOWN)
        ready = cores(packed, code)
        q_held, q_held_code = (p_far,), rows(0, (1,), *p_chips)
        p_held, p_held_chips = (), ()
    (p_last,), token = stage(
        lambda u, d: (jnp.concatenate([u, d], axis=1),), (p_up, p_down), ((8, D),), token
    )
    p_far = send(p_last, Y_SWAP)
    token = multiply(ready, token)
    (packed,), token = stage(
        lambda u, d, *h: (stack(*h, jnp.concatenate([u, d], axis=1)),),
        (q_up, q_down, p_last, *q_held, p_far),
        ((48, D),),
        token,
        1,
    )
    code = rows(0, (0,), 4) + q_held_code + rows(0, (1,), 4) + rows(1, (0, 1), 4)
    (_, near), (swapped, far) = cores(packed, code)
    sofar = last_rows(meta, codes + near, groups, packed, next_weight)
    return last_rows(meta, far, [], swapped, next_weight, sofar), updated


def solution(mesh):
    return jax.shard_map(
        local,
        mesh=mesh,
        in_specs=(
            P("dp", "tensor"),
            P("dp", None),
            P("dp", None),
            P("tensor", None),
            P("tensor", "dp", None),
            P(("dp", "tensor"), None),
            P(),
            P(None, "tensor"),
            P("dp"),
        ),
        out_specs=(P("dp", "tensor"), P(("dp", "tensor"), None)),
        check_vma=False,
    )
```

```python
import functools
import math

import jax
import jax.numpy as jnp
import numpy as np
from jax import lax
from jax.experimental import pallas as pl
from jax.experimental.pallas import tpu as pltpu
from jax.sharding import PartitionSpec as P

HD = 128
LEVELS = range(-13, -6)
F32 = jnp.float32
BF16 = jnp.bfloat16
D = 8192
HALF = D // 2
TILE = 2048
TILES = D // TILE

NY, NZ, NC = 2, 8, 2


def moves(step):
    def index(y, z, c):
        return (y * NZ + z) * NC + c

    return [
        (index(y, z, c), index(*step(y, z, c)))
        for y in range(NY)
        for z in range(NZ)
        for c in range(NC)
    ]


Z_UP = moves(lambda y, z, c: (y, (z + 1) % NZ, c))
Z_DOWN = moves(lambda y, z, c: (y, (z - 1) % NZ, c))
Y_SWAP = moves(lambda y, z, c: (1 - y, z, c))
C_SWAP = moves(lambda y, z, c: (y, z, 1 - c))


def send(value, step):
    return lax.ppermute(value, "tensor", step)


def row_code(piece, k, ky):
    return [((piece * 8 + k) * 2 + ky) * 8 + j for j in range(8)]


PAIRS = ((5, 3), (6, 2), (7, 1))
ORDER = (5, 3, 6, 2, 7, 1, 0)
CODES = (
    [v for k in (4, *ORDER) for v in row_code(0, k, 1)]
    + row_code(0, 4, 0)
    + row_code(1, 4, 0)
    + row_code(1, 4, 1)
    + [v for k in ORDER for v in row_code(0, k, 0)]
    + [v for k in ORDER for far in (0, 1) for v in row_code(1, k, far)]
)
ROWS = np.array(CODES, np.int32).reshape(1, 256)
SUMS = (24, 40, 8, 16, 16, 16, 16, 8, 32, 32, 32, 16)
SPLIT = 3


def placed(code, y, z, c):
    j, ky, k, piece = code & 7, (code >> 3) & 1, (code >> 4) & 7, code >> 7
    return (((ky ^ y) * NZ + ((k + z) & 7)) * NC + c) * 16 + piece * 8 + j


def sylvester(size):
    i = lax.broadcasted_iota(jnp.int32, (size, size), 0)
    j = lax.broadcasted_iota(jnp.int32, (size, size), 1)
    joined = i & j & 127
    for shift in (4, 2, 1):
        joined = joined ^ (joined >> shift)
    signs = 1 - 2 * (joined & 1)
    return jnp.where((i >> 7) == (j >> 7), signs, 0).astype(F32).astype(BF16)


def params(limit):
    return pltpu.CompilerParams(vmem_limit_bytes=limit << 20)


def cost(flops, moved, transcendentals=0):
    return pl.CostEstimate(
        flops=flops, bytes_accessed=moved, transcendentals=transcendentals
    )


ANY = pl.BlockSpec(memory_space=pl.ANY)
VMEM = pl.BlockSpec(memory_space=pltpu.VMEM)
TOKEN = jax.ShapeDtypeStruct((8, 128), F32)


A_COLS = 384


def attend_kernel(side, meta, docs, rows_ref, q_ref, e_ref, k_ref, v_ref, o_ref):
    key = lax.broadcasted_iota(jnp.int32, (1, 512), 1)
    at = pl.ds(pl.multiple_of(meta[3] * HD, HD), HD)
    keys, values = k_ref[:, at], v_ref[:, at]
    seg_k = jnp.zeros((1, 512), jnp.int32)
    end = jnp.int32(0)
    for i in range(4):
        end = end + docs[i]
        seg_k = seg_k + (key >= end).astype(jnp.int32)
    levels = e_ref[...].astype(F32).astype(BF16)
    codes = jnp.broadcast_to(rows_ref[...], (8, 256)).T[:, :1]
    where = placed(codes, meta[0], meta[1], meta[2] ^ side)
    seg_q = jnp.zeros((256, 1), jnp.int32)
    end = jnp.int32(0)
    for i in range(4):
        end = end + docs[i]
        seg_q = seg_q + (where >= end).astype(jnp.int32)
    allowed = (seg_q == seg_k) & (key <= where)
    pick = (where == key).astype(F32).astype(BF16)
    picked = jnp.dot(pick, q_ref[...], preferred_element_type=F32).astype(BF16)
    for head in range(2):
        scores = lax.dot_general(
            picked[:, head * HD : (head + 1) * HD],
            keys,
            (((1,), (1,)), ((), ())),
            preferred_element_type=F32,
        ) * HD ** (-0.5)
        scores = jnp.where(allowed, scores, F32(-1e30))
        top = jnp.max(scores, axis=1, keepdims=True)
        expo = jnp.where(allowed, jnp.exp(scores - top), F32(0.0))
        probs = (expo / jnp.sum(expo, axis=1, keepdims=True)).astype(BF16)
        out = jnp.dot(probs, values, preferred_element_type=F32).astype(BF16)
        o_ref[:, head * HD : (head + 1) * HD] = out
    level_of = lax.dot_general(
        pick, levels, (((1,), (1,)), ((), ())), preferred_element_type=F32
    )
    limit = jnp.zeros(level_of.shape, F32)
    for level in LEVELS:
        limit = limit + jnp.where(level_of == level, F32(448.0 * 2.0**level), F32(0.0))
    limit = jnp.concatenate([limit, jnp.zeros((256, 64), F32)], axis=1)
    o_ref[:, 256:] = limit.astype(BF16)


def attend(side, meta, docs, query, expo, keys, values):
    scalars = pl.BlockSpec(memory_space=pltpu.SMEM)
    shape = jax.ShapeDtypeStruct((256, A_COLS), BF16)
    return pl.pallas_call(
        functools.partial(attend_kernel, side),
        out_shape=shape,
        in_specs=[scalars, scalars] + [VMEM] * 5,
        out_specs=VMEM,
        compiler_params=params(16),
        cost_estimate=cost(3_000_000_000, 2_000_000, 300_000),
    )(meta, docs, jnp.asarray(ROWS), query, expo, keys, values)


CHUNK = 64


def turn_kernel(w_ref, left_ref, right_ref, buffer, result, in_sems, out_sems):
    parts = 256 // CHUNK
    copies, stores = [], []
    for i in range(parts):
        rows = pl.ds(i * CHUNK, CHUNK)
        copies.append(pltpu.make_async_copy(w_ref.at[rows], buffer.at[i], in_sems.at[i]))
        copies[i].start()
    table = sylvester(256)
    for i in range(parts):
        copies[i].wait()
        for half, o_ref in enumerate((left_ref, right_ref)):
            starts = range(half * HALF, (half + 1) * HALF, 256)
            blocks = jnp.concatenate([buffer[i, :, at : at + 256] for at in starts], axis=0)
            turned = jnp.dot(blocks, table, preferred_element_type=F32).astype(BF16)
            for n in range(HALF // 256):
                result[i, half, :, n * 256 : n * 256 + 256] = turned[
                    n * CHUNK : (n + 1) * CHUNK
                ]
            rows = pl.ds(i * CHUNK, CHUNK)
            stores.append(
                pltpu.make_async_copy(
                    result.at[i, half], o_ref.at[rows], out_sems.at[i, half]
                )
            )
            stores[-1].start()
    for store in stores:
        store.wait()


def turn(weight):
    parts = 256 // CHUNK
    shape = jax.ShapeDtypeStruct((256, HALF), BF16)
    hbm = pl.BlockSpec(memory_space=pltpu.HBM)
    return pl.pallas_call(
        turn_kernel,
        out_shape=(shape, shape),
        in_specs=[hbm],
        out_specs=(hbm, hbm),
        scratch_shapes=[
            pltpu.VMEM((parts, CHUNK, D), BF16),
            pltpu.VMEM((parts, 2, CHUNK, HALF), BF16),
            pltpu.SemaphoreType.DMA((parts,)),
            pltpu.SemaphoreType.DMA((parts, 2)),
        ],
        compiler_params=params(61),
        cost_estimate=cost(4_000_000_000, 8 << 20),
    )(weight)


def project_kernel(half, a_own, a_far, w_own, w_far, *refs):
    outs, bounds = refs[-1 - len(SUMS) : -1], refs[-1]
    tile = pl.program_id(0)
    wide = TILE // 128
    count = HALF // TILE

    @pl.when(tile == 0)
    def _():
        for side, a_ref in enumerate((a_own, a_far)):
            limits = a_ref[:, 256:].astype(F32) * F32(math.sqrt(128.0))
            for i in range(count):
                at = (half * count + i) * wide
                bounds[i, side] = limits[:, at : at + wide]

    for at in range(0, TILE, 256):
        terms = []
        for side, (a_ref, w_ref) in enumerate(((a_own, w_own), (a_far, w_far))):
            term = jnp.dot(
                a_ref[:, :256],
                w_ref[:, at : at + 256],
                preferred_element_type=F32,
            )
            for part in range(2):
                lane = at // 128 + part
                limit = jnp.broadcast_to(bounds[tile, side, :, lane : lane + 1], (256, 128))
                kept = term[:, part * 128 : part * 128 + 128]
                terms.append(jnp.maximum(jnp.minimum(kept, limit), -limit))
        total = jnp.concatenate([terms[0] + terms[2], terms[1] + terms[3]], axis=1)
        row = 0
        for o_ref in outs:
            count_rows = o_ref.shape[0]
            o_ref[:, at : at + 256] = total[row : row + count_rows].astype(BF16)
            row += count_rows


def project(half, a_own, a_far, w_own, w_far, sums=None):
    first = half * (HALF // TILE)
    here = pl.BlockSpec((256, TILE), lambda i: (0, i))
    shapes = [(count, HALF if at == SPLIT else D) for at, count in enumerate(SUMS)]
    maps = [
        (lambda i: (0, i)) if at == SPLIT else (lambda i: (0, i + first))
        for at in range(len(SUMS))
    ]
    given = [] if sums is None else [x for at, x in enumerate(sums) if at != SPLIT]
    into = [at for at in range(len(SUMS)) if at != SPLIT]
    return pl.pallas_call(
        functools.partial(project_kernel, half),
        out_shape=tuple(jax.ShapeDtypeStruct(s, BF16) for s in shapes),
        grid=(HALF // TILE,),
        in_specs=[
            pl.BlockSpec((256, A_COLS), lambda i: (0, 0)),
            pl.BlockSpec((256, A_COLS), lambda i: (0, 0)),
            here,
            here,
        ]
        + [ANY] * len(given),
        out_specs=tuple(pl.BlockSpec((s[0], TILE), m) for s, m in zip(shapes, maps)),
        scratch_shapes=[pltpu.VMEM((HALF // TILE, 2, 256, TILE // 128), F32)],
        input_output_aliases={4 + i: into[i] for i in range(len(given))},
        compiler_params=params(24),
        cost_estimate=cost(4_000_000_000, 6_500_000),
    )(a_own, a_far, w_own, w_far, *given)


def step_kernel(body, n_in, *refs):
    ins, outs, token = refs[:n_in], refs[n_in + 1 : -1], refs[-1]
    values = body(*[r[...].astype(F32) for r in ins])
    for o_ref, value in zip(outs, values):
        o_ref[...] = value.astype(o_ref.dtype)
    token[...] = jnp.zeros((8, 128), F32)


def stage(body, ins, outs, token, span=15):
    *results, token = pl.pallas_call(
        functools.partial(step_kernel, body, len(ins)),
        out_shape=tuple(jax.ShapeDtypeStruct(s, BF16) for s in outs) + (TOKEN,),
        in_specs=[VMEM] * len(ins) + [ANY],
        out_specs=(VMEM,) * (len(outs) + 1),
        compiler_params=params(24),
        cost_estimate=cost(span * 1_150_000_000, span * 3_600_000),
    )(*ins, token)
    return results, token


def finish(total, residual, gain):
    stacked = jnp.concatenate([total[:, b * 128 : b * 128 + 128] for b in range(64)], axis=0)
    table = sylvester(128)
    high = stacked.astype(BF16)
    low = (stacked - high.astype(F32)).astype(BF16)
    turned = jnp.dot(high, table, preferred_element_type=F32)
    turned = turned + jnp.dot(low, table, preferred_element_type=F32)
    turned = turned * F32(1.0 / 128.0)
    mixed = jnp.concatenate([turned[b * 8 : b * 8 + 8] for b in range(64)], axis=1)
    updated = residual + mixed
    inverse = lax.rsqrt(jnp.mean(updated * updated, axis=1, keepdims=True) + 1e-05)
    return updated * inverse * gain, updated


def halves(both, half_down, half_up):
    rows = half_down.shape[0]
    down, up = both[:rows], both[rows:]
    down = jnp.concatenate([down[:, :HALF] + half_down, down[:, HALF:]], axis=1)
    up = jnp.concatenate([up[:, :HALF], up[:, HALF:] + half_up], axis=1)
    return down, up


def times(x_refs, w_ref):
    total = None
    for at in range(0, D, 1024):
        rows = jnp.concatenate([x[:, at : at + 1024].astype(F32) for x in x_refs], axis=0)
        part = jnp.dot(
            rows.astype(BF16), w_ref[at : at + 1024, :], preferred_element_type=F32
        )
        total = part if total is None else total + part
    return total


def next_kernel(*refs):
    *x_refs, w_ref, _, o_ref, token = refs
    token[...] = jnp.zeros((8, 128), F32)
    o_ref[...] = times(x_refs, w_ref).astype(BF16)


def next_rows(chunks, weight, token):
    count = sum(x.shape[0] for x in chunks)
    return pl.pallas_call(
        next_kernel,
        out_shape=(jax.ShapeDtypeStruct((count, 256), BF16), TOKEN),
        in_specs=[VMEM] * (len(chunks) + 1) + [ANY],
        out_specs=(VMEM, VMEM),
        compiler_params=params(24),
        cost_estimate=cost(2 * count * D * 256, (4 << 20) + count * 16384),
    )(*chunks, weight, token)


def last_kernel(n_rows, n_groups, meta, code_ref, *refs):
    groups, x_refs = refs[:n_groups], refs[n_groups : n_groups + 1]
    w_ref, o_ref = refs[n_groups + 1], refs[-1]
    code = code_ref[...]
    target = placed(code & 255, meta[0], meta[1], (code >> 8) ^ meta[2])
    to = lax.broadcasted_iota(jnp.int32, (512, n_rows), 0)
    pick = (target == to).astype(F32).astype(BF16)
    rows = [x[...] for x in groups] + [times(x_refs, w_ref).astype(BF16)]
    rows = jnp.concatenate([x.astype(F32) for x in rows], axis=0).astype(BF16)
    value = jnp.dot(pick, rows, preferred_element_type=F32)
    if len(refs) > n_groups + 3:
        value = value + refs[n_groups + 2][...]
    o_ref[...] = value.astype(o_ref.dtype)


def last_rows(meta, codes, groups, chunk, weight, *sofar):
    table = np.array(codes, np.int32).reshape(1, -1)
    count = table.shape[1]
    return pl.pallas_call(
        functools.partial(last_kernel, count, len(groups)),
        out_shape=jax.ShapeDtypeStruct((512, 256), BF16 if sofar else F32),
        in_specs=[pl.BlockSpec(memory_space=pltpu.SMEM)]
        + [VMEM] * (len(groups) + 3 + len(sofar)),
        out_specs=VMEM,
        compiler_params=params(24),
        cost_estimate=cost(1_000_000_000, 6 << 20),
    )(meta, jnp.asarray(table), *groups, chunk, weight, *sofar)


def local(
    query, keys, values, out_weight, scale_exp, residual, norm_gain, next_weight, doc_lengths
):
    rank = lax.axis_index("tensor")
    meta = jnp.stack([rank >> 4, (rank >> 1) & 7, rank & 1, rank >> 2]).astype(jnp.int32)
    expo = scale_exp[0].T
    w_own = turn(out_weight)
    w_far = [send(w, C_SWAP) for w in w_own]
    given = (meta, doc_lengths, query, expo, keys, values)
    a_far = send(attend(1, *given), C_SWAP)
    a_own = attend(0, *given)
    sums = project(0, a_own, a_far, w_own[0], w_far[0])
    q_down = sums[SPLIT]
    sums = project(1, a_own, a_far, w_own[1], w_far[1], sums)
    p_send, p_later, p_own, q_up = sums[:4]
    p_owns, q_owns = sums[4:8], sums[8:12]
    gain = norm_gain.reshape(1, -1)

    token = jnp.zeros((8, 128), F32)
    q_down, q_up = send(q_down, Z_DOWN), send(q_up, Z_UP)
    p_got, p_rest = send(p_send, Y_SWAP), send(p_later, Y_SWAP)
    for step in range(4):
        if step < 3:
            q_body = halves if step == 0 else lambda a, d, u: (a[:16] + d, a[16:] + u)
            (q_down, q_up), token = stage(
                q_body, (q_owns[step], q_down, q_up), ((16, D), (16, D)), token
            )
            q_down, q_up = send(q_down, Z_DOWN), send(q_up, Z_UP)
        else:
            (q_near, q_send), token = stage(
                lambda a, d, u: ((a + d + u)[:8], (a + d + u)[8:]),
                (q_owns[3], q_down, q_up),
                ((8, D), (8, D)),
                token,
            )
        if step == 0:
            (p_down, p_up), token = stage(
                lambda a, b: ((a + b[:8])[:, :HALF], (a + b[:8])[:, HALF:]),
                (p_own, p_got),
                ((8, HALF), (8, HALF)),
                token,
            )
        else:
            at = step * 16 - 32
            if step == 1:
                p_body = lambda a, b, d, u: halves(a + b[8:], d, u)
            else:
                p_body = lambda a, b, d, u, at=at: (
                    a[:8] + b[at : at + 8] + d,
                    a[8:] + b[at + 8 : at + 16] + u,
                )
            (p_down, p_up), token = stage(
                p_body,
                (p_owns[step - 1], p_got if step == 1 else p_rest, p_down, p_up),
                ((8, D), (8, D)),
                token,
            )
        p_down, p_up = send(p_down, Z_DOWN), send(p_up, Z_UP)
    q_got = send(q_send, Y_SWAP)
    (q_norm, q_updated), token = stage(
        lambda a, b, r, g: finish(a + b, r, g),
        (q_near, q_got, residual[8:], gain),
        ((8, D), (8, D)),
        token,
    )
    (p_norm, p_updated), token = stage(
        lambda a, b, d, u, r, g: finish(a + b[32:] + d + u, r, g),
        (p_owns[3], p_rest, p_down, p_up, residual[:8], gain),
        ((8, D), (8, D)),
        token,
    )

    groups, codes = [], []

    def multiply(chunks, token):
        rows, token = next_rows([x for x, _ in chunks], next_weight, token)
        groups.append(rows)
        for _, code in chunks:
            codes.extend(code)
        return token

    def cores(value, code):
        return [(value, code), (send(value, C_SWAP), [256 + v for v in code])]

    def rows(piece, far, *chips):
        return [v for k in chips for ky in far for v in row_code(piece, k, ky)]

    def stack(*parts):
        return jnp.concatenate(parts, axis=0)

    p_up, p_down = send(p_norm, Z_UP), send(p_norm, Z_DOWN)
    q_far = send(q_norm, Y_SWAP)
    (q_pair,), token = stage(lambda a, b: (stack(a, b),), (q_norm, q_far), ((16, D),), token, 1)
    q_up, q_down = send(q_pair, Z_UP), send(q_pair, Z_DOWN)
    p_held, p_held_chips = (p_norm,), (0,)
    q_held, q_held_code = (q_pair,), rows(1, (0, 1), 0)
    ready = None
    for hop in range(1, 4):
        chips = (8 - hop, hop)
        count = 8 * len(p_held) + 16
        (p_up, p_down, p_both), token = stage(
            lambda u, d, *h: (u, d, stack(*h, u, d)),
            (p_up, p_down, *p_held),
            ((8, D), (8, D), (count, D)),
            token,
        )
        if hop == 1:
            (updated,), token = stage(
                lambda a, b: (stack(a, b),), (p_updated, q_updated), ((16, D),), token, 1
            )
        p_chips = p_held_chips + chips
        if hop < 3:
            p_up, p_down = send(p_up, Z_UP), send(p_down, Z_DOWN)
        else:
            p_up, p_down = send(p_up[:, :HALF], Z_UP), send(p_down[:, HALF:], Z_DOWN)
        p_far = send(p_both, Y_SWAP)
        if ready is not None:
            token = multiply(ready, token)
        whole = (p_both, *q_held)
        (q_up, q_down, packed), token = stage(
            lambda u, d, *h: (u, d, stack(*h, u, d)),
            (q_up, q_down, *whole),
            ((16, D), (16, D), (32 + sum(x.shape[0] for x in whole), D)),
            token,
        )
        code = rows(0, (0,), *p_chips) + q_held_code + rows(1, (0, 1), *chips)
        if hop < 3:
            q_up, q_down = send(q_up, Z_UP), send(q_down, Z_DOWN)
        else:
            q_up, q_down = send(q_up[:, :HALF], Z_UP), send(q_down[:, HALF:], Z_DOWN)
        ready = cores(packed, code)
        q_held, q_held_code = (p_far,), rows(0, (1,), *p_chips)
        p_held, p_held_chips = (), ()
    (p_last,), token = stage(
        lambda u, d: (jnp.concatenate([u, d], axis=1),), (p_up, p_down), ((8, D),), token
    )
    p_far = send(p_last, Y_SWAP)
    token = multiply(ready, token)
    (packed,), token = stage(
        lambda u, d, *h: (stack(*h, jnp.concatenate([u, d], axis=1)),),
        (q_up, q_down, p_last, *q_held, p_far),
        ((48, D),),
        token,
        1,
    )
    code = rows(0, (0,), 4) + q_held_code + rows(0, (1,), 4) + rows(1, (0, 1), 4)
    (_, near), (swapped, far) = cores(packed, code)
    sofar = last_rows(meta, codes + near, groups, packed, next_weight)
    return last_rows(meta, far, [], swapped, next_weight, sofar), updated


def solution(mesh):
    return jax.shard_map(
        local,
        mesh=mesh,
        in_specs=(
            P("dp", "tensor"),
            P("dp", None),
            P("dp", None),
            P("tensor", None),
            P("tensor", "dp", None),
            P(("dp", "tensor"), None),
            P(),
            P(None, "tensor"),
            P("dp"),
        ),
        out_specs=(P("dp", "tensor"), P(("dp", "tensor"), None)),
        check_vma=False,
    )
```

```python
import functools
import math

import jax
import jax.numpy as jnp
import numpy as np
from jax import lax
from jax.experimental import pallas as pl
from jax.experimental.pallas import tpu as pltpu
from jax.sharding import PartitionSpec as P

HD = 128
LEVELS = range(-13, -6)
F32 = jnp.float32
BF16 = jnp.bfloat16
D = 8192
HALF = D // 2
TILE = 2048
TILES = D // TILE

NY, NZ, NC = 2, 8, 2


def moves(step):
    def index(y, z, c):
        return (y * NZ + z) * NC + c

    return [
        (index(y, z, c), index(*step(y, z, c)))
        for y in range(NY)
        for z in range(NZ)
        for c in range(NC)
    ]


Z_UP = moves(lambda y, z, c: (y, (z + 1) % NZ, c))
Z_DOWN = moves(lambda y, z, c: (y, (z - 1) % NZ, c))
Y_SWAP = moves(lambda y, z, c: (1 - y, z, c))
C_SWAP = moves(lambda y, z, c: (y, z, 1 - c))


def send(value, step):
    return lax.ppermute(value, "tensor", step)


def row_code(piece, k, ky):
    return [((piece * 8 + k) * 2 + ky) * 8 + j for j in range(8)]


PAIRS = ((5, 3), (6, 2), (7, 1))
ORDER = (5, 3, 6, 2, 7, 1, 0)
CODES = (
    [v for k in (4, *ORDER) for v in row_code(0, k, 1)]
    + row_code(0, 4, 0)
    + row_code(1, 4, 0)
    + row_code(1, 4, 1)
    + [v for k in ORDER for v in row_code(0, k, 0)]
    + [v for k in ORDER for far in (0, 1) for v in row_code(1, k, far)]
)
ROWS = np.array(CODES, np.int32).reshape(1, 256)
SUMS = (8, 32, 24, 8, 16, 16, 16, 16, 8, 32, 32, 32, 16)
SPLIT = 4


def placed(code, y, z, c):
    j, ky, k, piece = code & 7, (code >> 3) & 1, (code >> 4) & 7, code >> 7
    return (((ky ^ y) * NZ + ((k + z) & 7)) * NC + c) * 16 + piece * 8 + j


def sylvester(size):
    i = lax.broadcasted_iota(jnp.int32, (size, size), 0)
    j = lax.broadcasted_iota(jnp.int32, (size, size), 1)
    joined = i & j & 127
    for shift in (4, 2, 1):
        joined = joined ^ (joined >> shift)
    signs = 1 - 2 * (joined & 1)
    return jnp.where((i >> 7) == (j >> 7), signs, 0).astype(F32).astype(BF16)


def params(limit):
    return pltpu.CompilerParams(vmem_limit_bytes=limit << 20)


def cost(flops, moved, transcendentals=0):
    return pl.CostEstimate(
        flops=flops, bytes_accessed=moved, transcendentals=transcendentals
    )


ANY = pl.BlockSpec(memory_space=pl.ANY)
VMEM = pl.BlockSpec(memory_space=pltpu.VMEM)
TOKEN = jax.ShapeDtypeStruct((8, 128), F32)


A_COLS = 384


def attend_kernel(side, meta, docs, rows_ref, q_ref, e_ref, k_ref, v_ref, o_ref):
    key = lax.broadcasted_iota(jnp.int32, (1, 512), 1)
    at = pl.ds(pl.multiple_of(meta[3] * HD, HD), HD)
    keys, values = k_ref[:, at], v_ref[:, at]
    seg_k = jnp.zeros((1, 512), jnp.int32)
    end = jnp.int32(0)
    for i in range(4):
        end = end + docs[i]
        seg_k = seg_k + (key >= end).astype(jnp.int32)
    levels = e_ref[...].astype(F32).astype(BF16)
    codes = jnp.broadcast_to(rows_ref[...], (8, 256)).T[:, :1]
    where = placed(codes, meta[0], meta[1], meta[2] ^ side)
    seg_q = jnp.zeros((256, 1), jnp.int32)
    end = jnp.int32(0)
    for i in range(4):
        end = end + docs[i]
        seg_q = seg_q + (where >= end).astype(jnp.int32)
    allowed = (seg_q == seg_k) & (key <= where)
    pick = (where == key).astype(F32).astype(BF16)
    picked = jnp.dot(pick, q_ref[...], preferred_element_type=F32).astype(BF16)
    for head in range(2):
        scores = lax.dot_general(
            picked[:, head * HD : (head + 1) * HD],
            keys,
            (((1,), (1,)), ((), ())),
            preferred_element_type=F32,
        ) * HD ** (-0.5)
        scores = jnp.where(allowed, scores, F32(-1e30))
        top = jnp.max(scores, axis=1, keepdims=True)
        expo = jnp.where(allowed, jnp.exp(scores - top), F32(0.0))
        probs = (expo / jnp.sum(expo, axis=1, keepdims=True)).astype(BF16)
        out = jnp.dot(probs, values, preferred_element_type=F32).astype(BF16)
        o_ref[:, head * HD : (head + 1) * HD] = out
    level_of = lax.dot_general(
        pick, levels, (((1,), (1,)), ((), ())), preferred_element_type=F32
    )
    limit = jnp.zeros(level_of.shape, F32)
    for level in LEVELS:
        limit = limit + jnp.where(level_of == level, F32(448.0 * 2.0**level), F32(0.0))
    limit = jnp.concatenate([limit, jnp.zeros((256, 64), F32)], axis=1)
    o_ref[:, 256:] = limit.astype(BF16)


def attend(side, meta, docs, query, expo, keys, values):
    scalars = pl.BlockSpec(memory_space=pltpu.SMEM)
    shape = jax.ShapeDtypeStruct((256, A_COLS), BF16)
    return pl.pallas_call(
        functools.partial(attend_kernel, side),
        out_shape=shape,
        in_specs=[scalars, scalars] + [VMEM] * 5,
        out_specs=VMEM,
        compiler_params=params(16),
        cost_estimate=cost(3_000_000_000, 2_000_000, 300_000),
    )(meta, docs, jnp.asarray(ROWS), query, expo, keys, values)


CHUNK = 64


def turn_kernel(w_ref, left_ref, right_ref, buffer, result, in_sems, out_sems):
    parts = 256 // CHUNK
    copies, stores = [], []
    for i in range(parts):
        rows = pl.ds(i * CHUNK, CHUNK)
        copies.append(pltpu.make_async_copy(w_ref.at[rows], buffer.at[i], in_sems.at[i]))
        copies[i].start()
    table = sylvester(256)
    for i in range(parts):
        copies[i].wait()
        for half, o_ref in enumerate((left_ref, right_ref)):
            starts = range(half * HALF, (half + 1) * HALF, 256)
            blocks = jnp.concatenate([buffer[i, :, at : at + 256] for at in starts], axis=0)
            turned = jnp.dot(blocks, table, preferred_element_type=F32).astype(BF16)
            for n in range(HALF // 256):
                result[i, half, :, n * 256 : n * 256 + 256] = turned[
                    n * CHUNK : (n + 1) * CHUNK
                ]
            rows = pl.ds(i * CHUNK, CHUNK)
            stores.append(
                pltpu.make_async_copy(
                    result.at[i, half], o_ref.at[rows], out_sems.at[i, half]
                )
            )
            stores[-1].start()
    for store in stores:
        store.wait()


def turn(weight):
    parts = 256 // CHUNK
    shape = jax.ShapeDtypeStruct((256, HALF), BF16)
    hbm = pl.BlockSpec(memory_space=pltpu.HBM)
    return pl.pallas_call(
        turn_kernel,
        out_shape=(shape, shape),
        in_specs=[hbm],
        out_specs=(hbm, hbm),
        scratch_shapes=[
            pltpu.VMEM((parts, CHUNK, D), BF16),
            pltpu.VMEM((parts, 2, CHUNK, HALF), BF16),
            pltpu.SemaphoreType.DMA((parts,)),
            pltpu.SemaphoreType.DMA((parts, 2)),
        ],
        compiler_params=params(61),
        cost_estimate=cost(4_000_000_000, 8 << 20),
    )(weight)


def project_kernel(half, a_own, a_far, w_own, w_far, *refs):
    outs, bounds = refs[-1 - len(SUMS) : -1], refs[-1]
    tile = pl.program_id(0)
    wide = TILE // 128
    count = HALF // TILE

    @pl.when(tile == 0)
    def _():
        for side, a_ref in enumerate((a_own, a_far)):
            limits = a_ref[:, 256:].astype(F32) * F32(math.sqrt(128.0))
            for i in range(count):
                at = (half * count + i) * wide
                bounds[i, side] = limits[:, at : at + wide]

    for at in range(0, TILE, 256):
        terms = []
        for side, (a_ref, w_ref) in enumerate(((a_own, w_own), (a_far, w_far))):
            term = jnp.dot(
                a_ref[:, :256],
                w_ref[:, at : at + 256],
                preferred_element_type=F32,
            )
            for part in range(2):
                lane = at // 128 + part
                limit = jnp.broadcast_to(bounds[tile, side, :, lane : lane + 1], (256, 128))
                kept = term[:, part * 128 : part * 128 + 128]
                terms.append(jnp.maximum(jnp.minimum(kept, limit), -limit))
        total = jnp.concatenate([terms[0] + terms[2], terms[1] + terms[3]], axis=1)
        row = 0
        for o_ref in outs:
            count_rows = o_ref.shape[0]
            o_ref[:, at : at + 256] = total[row : row + count_rows].astype(BF16)
            row += count_rows


def project(half, a_own, a_far, w_own, w_far, sums=None):
    first = half * (HALF // TILE)
    here = pl.BlockSpec((256, TILE), lambda i: (0, i))
    shapes = [(count, HALF if at == SPLIT else D) for at, count in enumerate(SUMS)]
    maps = [
        (lambda i: (0, i)) if at == SPLIT else (lambda i: (0, i + first))
        for at in range(len(SUMS))
    ]
    given = [] if sums is None else [x for at, x in enumerate(sums) if at != SPLIT]
    into = [at for at in range(len(SUMS)) if at != SPLIT]
    return pl.pallas_call(
        functools.partial(project_kernel, half),
        out_shape=tuple(jax.ShapeDtypeStruct(s, BF16) for s in shapes),
        grid=(HALF // TILE,),
        in_specs=[
            pl.BlockSpec((256, A_COLS), lambda i: (0, 0)),
            pl.BlockSpec((256, A_COLS), lambda i: (0, 0)),
            here,
            here,
        ]
        + [ANY] * len(given),
        out_specs=tuple(pl.BlockSpec((s[0], TILE), m) for s, m in zip(shapes, maps)),
        scratch_shapes=[pltpu.VMEM((HALF // TILE, 2, 256, TILE // 128), F32)],
        input_output_aliases={4 + i: into[i] for i in range(len(given))},
        compiler_params=params(24),
        cost_estimate=cost(4_000_000_000, 6_500_000),
    )(a_own, a_far, w_own, w_far, *given)


def step_kernel(body, n_in, *refs):
    ins, outs, token = refs[:n_in], refs[n_in + 1 : -1], refs[-1]
    values = body(*[r[...].astype(F32) for r in ins])
    for o_ref, value in zip(outs, values):
        o_ref[...] = value.astype(o_ref.dtype)
    token[...] = jnp.zeros((8, 128), F32)


def stage(body, ins, outs, token, span=15):
    *results, token = pl.pallas_call(
        functools.partial(step_kernel, body, len(ins)),
        out_shape=tuple(jax.ShapeDtypeStruct(s, BF16) for s in outs) + (TOKEN,),
        in_specs=[VMEM] * len(ins) + [ANY],
        out_specs=(VMEM,) * (len(outs) + 1),
        compiler_params=params(24),
        cost_estimate=cost(span * 1_150_000_000, span * 3_600_000),
    )(*ins, token)
    return results, token


def finish(total, residual, gain):
    stacked = jnp.concatenate([total[:, b * 128 : b * 128 + 128] for b in range(64)], axis=0)
    table = sylvester(128)
    high = stacked.astype(BF16)
    low = (stacked - high.astype(F32)).astype(BF16)
    turned = jnp.dot(high, table, preferred_element_type=F32)
    turned = turned + jnp.dot(low, table, preferred_element_type=F32)
    turned = turned * F32(1.0 / 128.0)
    mixed = jnp.concatenate([turned[b * 8 : b * 8 + 8] for b in range(64)], axis=1)
    updated = residual + mixed
    inverse = lax.rsqrt(jnp.mean(updated * updated, axis=1, keepdims=True) + 1e-05)
    return updated * inverse * gain, updated


def halves(both, half_down, half_up):
    rows = half_down.shape[0]
    down, up = both[:rows], both[rows:]
    down = jnp.concatenate([down[:, :HALF] + half_down, down[:, HALF:]], axis=1)
    up = jnp.concatenate([up[:, :HALF], up[:, HALF:] + half_up], axis=1)
    return down, up


def times(x_refs, w_ref):
    total = None
    for at in range(0, D, 1024):
        rows = jnp.concatenate([x[:, at : at + 1024].astype(F32) for x in x_refs], axis=0)
        part = jnp.dot(
            rows.astype(BF16), w_ref[at : at + 1024, :], preferred_element_type=F32
        )
        total = part if total is None else total + part
    return total


def next_kernel(*refs):
    *x_refs, w_ref, _, o_ref, token = refs
    token[...] = jnp.zeros((8, 128), F32)
    o_ref[...] = times(x_refs, w_ref).astype(BF16)


def next_rows(chunks, weight, token):
    count = sum(x.shape[0] for x in chunks)
    return pl.pallas_call(
        next_kernel,
        out_shape=(jax.ShapeDtypeStruct((count, 256), BF16), TOKEN),
        in_specs=[VMEM] * (len(chunks) + 1) + [ANY],
        out_specs=(VMEM, VMEM),
        compiler_params=params(24),
        cost_estimate=cost(2 * count * D * 256, (4 << 20) + count * 16384),
    )(*chunks, weight, token)


def last_kernel(n_rows, n_groups, meta, code_ref, *refs):
    groups, x_refs = refs[:n_groups], refs[n_groups : n_groups + 1]
    w_ref, o_ref = refs[n_groups + 1], refs[-1]
    code = code_ref[...]
    target = placed(code & 255, meta[0], meta[1], (code >> 8) ^ meta[2])
    to = lax.broadcasted_iota(jnp.int32, (512, n_rows), 0)
    pick = (target == to).astype(F32).astype(BF16)
    rows = [x[...] for x in groups] + [times(x_refs, w_ref).astype(BF16)]
    rows = jnp.concatenate([x.astype(F32) for x in rows], axis=0).astype(BF16)
    value = jnp.dot(pick, rows, preferred_element_type=F32)
    if len(refs) > n_groups + 3:
        value = value + refs[n_groups + 2][...]
    o_ref[...] = value.astype(o_ref.dtype)


def last_rows(meta, codes, groups, chunk, weight, *sofar):
    table = np.array(codes, np.int32).reshape(1, -1)
    count = table.shape[1]
    return pl.pallas_call(
        functools.partial(last_kernel, count, len(groups)),
        out_shape=jax.ShapeDtypeStruct((512, 256), BF16 if sofar else F32),
        in_specs=[pl.BlockSpec(memory_space=pltpu.SMEM)]
        + [VMEM] * (len(groups) + 3 + len(sofar)),
        out_specs=VMEM,
        compiler_params=params(24),
        cost_estimate=cost(1_000_000_000, 6 << 20),
    )(meta, jnp.asarray(table), *groups, chunk, weight, *sofar)


def local(
    query, keys, values, out_weight, scale_exp, residual, norm_gain, next_weight, doc_lengths
):
    rank = lax.axis_index("tensor")
    meta = jnp.stack([rank >> 4, (rank >> 1) & 7, rank & 1, rank >> 2]).astype(jnp.int32)
    expo = scale_exp[0].T
    w_own = turn(out_weight)
    w_far = [send(w, C_SWAP) for w in w_own]
    given = (meta, doc_lengths, query, expo, keys, values)
    a_far = send(attend(1, *given), C_SWAP)
    a_own = attend(0, *given)
    sums = project(0, a_own, a_far, w_own[0], w_far[0])
    q_down = sums[SPLIT]
    sums = project(1, a_own, a_far, w_own[1], w_far[1], sums)
    *p_sends, p_own, q_up = sums[:5]
    p_owns, q_owns = sums[5:9], sums[9:13]
    gain = norm_gain.reshape(1, -1)

    token = jnp.zeros((8, 128), F32)
    q_down, q_up = send(q_down, Z_DOWN), send(q_up, Z_UP)
    p_got, p_mid = send(p_sends[0], Y_SWAP), send(p_sends[1], Y_SWAP)
    (p_down, p_up), token = stage(
        lambda a, b: ((a + b)[:, :HALF], (a + b)[:, HALF:]),
        (p_own, p_got),
        ((8, HALF), (8, HALF)),
        token,
    )
    p_down, p_up = send(p_down, Z_DOWN), send(p_up, Z_UP)
    for step in range(3):
        if step == 0:
            q_body = halves
            p_body = lambda a, b, d, u: halves(a + b[:16], d, u)
        else:
            q_body = lambda a, d, u: (a[:16] + d, a[16:] + u)
            at = 16 if step == 1 else 0
            p_body = lambda a, b, d, u, at=at: (
                a[:8] + b[at : at + 8] + d,
                a[8:] + b[at + 8 : at + 16] + u,
            )
        (q_down, q_up), token = stage(
            q_body, (q_owns[step], q_down, q_up), ((16, D), (16, D)), token
        )
        q_down, q_up = send(q_down, Z_DOWN), send(q_up, Z_UP)
        (p_down, p_up), token = stage(
            p_body,
            (p_owns[step], p_mid if step < 2 else p_rest, p_down, p_up),
            ((8, D), (8, D)),
            token,
        )
        if step == 0:
            later, p_down = lax.optimization_barrier((p_sends[2], p_down))
            p_rest = send(later, Y_SWAP)
        p_down, p_up = send(p_down, Z_DOWN), send(p_up, Z_UP)
    (q_sum,), token = stage(
        lambda a, d, u: (a + d + u,), (q_owns[3], q_down, q_up), ((16, D),), token
    )
    q_got = send(q_sum, Y_SWAP)
    own_residual, q_sum = lax.optimization_barrier((residual[8:], q_sum))
    far_residual = send(own_residual, Y_SWAP)
    (p_norm, p_updated), token = stage(
        lambda a, b, d, u, r, g: finish(a + b[16:] + d + u, r, g),
        (p_owns[3], p_rest, p_down, p_up, residual[:8], gain),
        ((8, D), (8, D)),
        token,
    )
    def finish_pair(a, b, r, far_r, g):
        near, updated = finish(a[:8] + b[8:], r, g)
        far, _ = finish(a[8:] + b[:8], far_r, g)
        return jnp.concatenate([near, far], axis=0), updated

    (q_pair, q_updated), token = stage(
        finish_pair,
        (q_sum, q_got, residual[8:], far_residual, gain),
        ((16, D), (8, D)),
        token,
    )

    groups, codes = [], []

    def multiply(chunks, token):
        rows, token = next_rows([x for x, _ in chunks], next_weight, token)
        groups.append(rows)
        for _, code in chunks:
            codes.extend(code)
        return token

    def cores(value, code):
        return [(value, code), (send(value, C_SWAP), [256 + v for v in code])]

    def rows(piece, far, *chips):
        return [v for k in chips for ky in far for v in row_code(piece, k, ky)]

    def stack(*parts):
        return jnp.concatenate(parts, axis=0)

    p_up, p_down = send(p_norm, Z_UP), send(p_norm, Z_DOWN)
    q_up, q_down = send(q_pair, Z_UP), send(q_pair, Z_DOWN)
    p_held, p_held_chips = (p_norm,), (0,)
    q_held, q_held_code = (q_pair,), rows(1, (0, 1), 0)
    ready = None
    for hop in range(1, 4):
        chips = (8 - hop, hop)
        count = 8 * len(p_held) + 16
        (p_up, p_down, p_both), token = stage(
            lambda u, d, *h: (u, d, stack(*h, u, d)),
            (p_up, p_down, *p_held),
            ((8, D), (8, D), (count, D)),
            token,
        )
        if hop == 1:
            (updated,), token = stage(
                lambda a, b: (stack(a, b),), (p_updated, q_updated), ((16, D),), token, 1
            )
        p_chips = p_held_chips + chips
        if hop < 3:
            p_up, p_down = send(p_up, Z_UP), send(p_down, Z_DOWN)
        else:
            p_up, p_down = send(p_up[:, :HALF], Z_UP), send(p_down[:, HALF:], Z_DOWN)
        p_far = send(p_both, Y_SWAP)
        if ready is not None:
            token = multiply(ready, token)
        whole = (p_both, *q_held)
        (q_up, q_down, packed), token = stage(
            lambda u, d, *h: (u, d, stack(*h, u, d)),
            (q_up, q_down, *whole),
            ((16, D), (16, D), (32 + sum(x.shape[0] for x in whole), D)),
            token,
        )
        code = rows(0, (0,), *p_chips) + q_held_code + rows(1, (0, 1), *chips)
        if hop < 3:
            q_up, q_down = send(q_up, Z_UP), send(q_down, Z_DOWN)
        else:
            q_up, q_down = send(q_up[:, :HALF], Z_UP), send(q_down[:, HALF:], Z_DOWN)
        ready = cores(packed, code)
        q_held, q_held_code = (p_far,), rows(0, (1,), *p_chips)
        p_held, p_held_chips = (), ()
    (p_last,), token = stage(
        lambda u, d: (jnp.concatenate([u, d], axis=1),), (p_up, p_down), ((8, D),), token
    )
    p_far = send(p_last, Y_SWAP)
    token = multiply(ready, token)
    (packed,), token = stage(
        lambda u, d, *h: (stack(*h, jnp.concatenate([u, d], axis=1)),),
        (q_up, q_down, p_last, *q_held, p_far),
        ((48, D),),
        token,
        1,
    )
    code = rows(0, (0,), 4) + q_held_code + rows(0, (1,), 4) + rows(1, (0, 1), 4)
    (_, near), (swapped, far) = cores(packed, code)
    sofar = last_rows(meta, codes + near, groups, packed, next_weight)
    return last_rows(meta, far, [], swapped, next_weight, sofar), updated


def solution(mesh):
    return jax.shard_map(
        local,
        mesh=mesh,
        in_specs=(
            P("dp", "tensor"),
            P("dp", None),
            P("dp", None),
            P("tensor", None),
            P("tensor", "dp", None),
            P(("dp", "tensor"), None),
            P(),
            P(None, "tensor"),
            P("dp"),
        ),
        out_specs=(P("dp", "tensor"), P(("dp", "tensor"), None)),
        check_vma=False,
    )
```

```python
import functools
import math

import jax
import jax.numpy as jnp
import numpy as np
from jax import lax
from jax.experimental import pallas as pl
from jax.experimental.pallas import tpu as pltpu
from jax.sharding import PartitionSpec as P

HD = 128
LEVELS = range(-13, -6)
F32 = jnp.float32
BF16 = jnp.bfloat16
D = 8192
HALF = D // 2
TILE = 2048
TILES = D // TILE

NY, NZ, NC = 2, 8, 2


def moves(step):
    def index(y, z, c):
        return (y * NZ + z) * NC + c

    return [
        (index(y, z, c), index(*step(y, z, c)))
        for y in range(NY)
        for z in range(NZ)
        for c in range(NC)
    ]


Z_UP = moves(lambda y, z, c: (y, (z + 1) % NZ, c))
Z_DOWN = moves(lambda y, z, c: (y, (z - 1) % NZ, c))
Y_SWAP = moves(lambda y, z, c: (1 - y, z, c))
C_SWAP = moves(lambda y, z, c: (y, z, 1 - c))


def send(value, step):
    return lax.ppermute(value, "tensor", step)


def row_code(piece, k, ky):
    return [((piece * 8 + k) * 2 + ky) * 8 + j for j in range(8)]


PAIRS = ((5, 3), (6, 2), (7, 1))
ORDER = (5, 3, 6, 2, 7, 1, 0)
CODES = (
    [v for k in (4, *ORDER) for v in row_code(0, k, 1)]
    + row_code(0, 4, 0)
    + row_code(1, 4, 0)
    + row_code(1, 4, 1)
    + [v for k in ORDER for v in row_code(0, k, 0)]
    + [v for k in ORDER for far in (0, 1) for v in row_code(1, k, far)]
)
ROWS = np.array(CODES, np.int32).reshape(1, 256)
SUMS = (8, 32, 24, 8, 16, 16, 16, 16, 8, 32, 32, 32, 16)
SPLIT = 4


def placed(code, y, z, c):
    j, ky, k, piece = code & 7, (code >> 3) & 1, (code >> 4) & 7, code >> 7
    return (((ky ^ y) * NZ + ((k + z) & 7)) * NC + c) * 16 + piece * 8 + j


def sylvester(size):
    i = lax.broadcasted_iota(jnp.int32, (size, size), 0)
    j = lax.broadcasted_iota(jnp.int32, (size, size), 1)
    joined = i & j & 127
    for shift in (4, 2, 1):
        joined = joined ^ (joined >> shift)
    signs = 1 - 2 * (joined & 1)
    return jnp.where((i >> 7) == (j >> 7), signs, 0).astype(F32).astype(BF16)


def params(limit):
    return pltpu.CompilerParams(vmem_limit_bytes=limit << 20)


def cost(flops, moved, transcendentals=0):
    return pl.CostEstimate(
        flops=flops, bytes_accessed=moved, transcendentals=transcendentals
    )


ANY = pl.BlockSpec(memory_space=pl.ANY)
VMEM = pl.BlockSpec(memory_space=pltpu.VMEM)
TOKEN = jax.ShapeDtypeStruct((8, 128), F32)


A_COLS = 384


def attend_kernel(side, meta, docs, rows_ref, q_ref, e_ref, k_ref, v_ref, o_ref):
    key = lax.broadcasted_iota(jnp.int32, (1, 512), 1)
    at = pl.ds(pl.multiple_of(meta[3] * HD, HD), HD)
    keys, values = k_ref[:, at], v_ref[:, at]
    seg_k = jnp.zeros((1, 512), jnp.int32)
    end = jnp.int32(0)
    for i in range(4):
        end = end + docs[i]
        seg_k = seg_k + (key >= end).astype(jnp.int32)
    levels = e_ref[...].astype(F32).astype(BF16)
    codes = jnp.broadcast_to(rows_ref[...], (8, 256)).T[:, :1]
    where = placed(codes, meta[0], meta[1], meta[2] ^ side)
    seg_q = jnp.zeros((256, 1), jnp.int32)
    end = jnp.int32(0)
    for i in range(4):
        end = end + docs[i]
        seg_q = seg_q + (where >= end).astype(jnp.int32)
    allowed = (seg_q == seg_k) & (key <= where)
    pick = (where == key).astype(F32).astype(BF16)
    picked = jnp.dot(pick, q_ref[...], preferred_element_type=F32).astype(BF16)
    for head in range(2):
        scores = lax.dot_general(
            picked[:, head * HD : (head + 1) * HD],
            keys,
            (((1,), (1,)), ((), ())),
            preferred_element_type=F32,
        ) * HD ** (-0.5)
        scores = jnp.where(allowed, scores, F32(-1e30))
        top = jnp.max(scores, axis=1, keepdims=True)
        expo = jnp.where(allowed, jnp.exp(scores - top), F32(0.0))
        probs = (expo / jnp.sum(expo, axis=1, keepdims=True)).astype(BF16)
        out = jnp.dot(probs, values, preferred_element_type=F32).astype(BF16)
        o_ref[:, head * HD : (head + 1) * HD] = out
    level_of = lax.dot_general(
        pick, levels, (((1,), (1,)), ((), ())), preferred_element_type=F32
    )
    limit = jnp.zeros(level_of.shape, F32)
    for level in LEVELS:
        limit = limit + jnp.where(level_of == level, F32(448.0 * 2.0**level), F32(0.0))
    limit = jnp.concatenate([limit, jnp.zeros((256, 64), F32)], axis=1)
    o_ref[:, 256:] = limit.astype(BF16)


def attend(side, meta, docs, query, expo, keys, values):
    scalars = pl.BlockSpec(memory_space=pltpu.SMEM)
    shape = jax.ShapeDtypeStruct((256, A_COLS), BF16)
    return pl.pallas_call(
        functools.partial(attend_kernel, side),
        out_shape=shape,
        in_specs=[scalars, scalars] + [VMEM] * 5,
        out_specs=VMEM,
        compiler_params=params(16),
        cost_estimate=cost(3_000_000_000, 2_000_000, 300_000),
    )(meta, docs, jnp.asarray(ROWS), query, expo, keys, values)


CHUNK = 64


def turn_kernel(w_ref, left_ref, right_ref, buffer, result, in_sems, out_sems):
    parts = 256 // CHUNK
    copies, stores = [], []
    for i in range(parts):
        rows = pl.ds(i * CHUNK, CHUNK)
        copies.append(pltpu.make_async_copy(w_ref.at[rows], buffer.at[i], in_sems.at[i]))
        copies[i].start()
    table = sylvester(256)
    for i in range(parts):
        copies[i].wait()
        for half, o_ref in enumerate((left_ref, right_ref)):
            starts = range(half * HALF, (half + 1) * HALF, 256)
            blocks = jnp.concatenate([buffer[i, :, at : at + 256] for at in starts], axis=0)
            turned = jnp.dot(blocks, table, preferred_element_type=F32).astype(BF16)
            for n in range(HALF // 256):
                result[i, half, :, n * 256 : n * 256 + 256] = turned[
                    n * CHUNK : (n + 1) * CHUNK
                ]
            rows = pl.ds(i * CHUNK, CHUNK)
            stores.append(
                pltpu.make_async_copy(
                    result.at[i, half], o_ref.at[rows], out_sems.at[i, half]
                )
            )
            stores[-1].start()
    for store in stores:
        store.wait()


def turn(weight):
    parts = 256 // CHUNK
    shape = jax.ShapeDtypeStruct((256, HALF), BF16)
    hbm = pl.BlockSpec(memory_space=pltpu.HBM)
    return pl.pallas_call(
        turn_kernel,
        out_shape=(shape, shape),
        in_specs=[hbm],
        out_specs=(hbm, hbm),
        scratch_shapes=[
            pltpu.VMEM((parts, CHUNK, D), BF16),
            pltpu.VMEM((parts, 2, CHUNK, HALF), BF16),
            pltpu.SemaphoreType.DMA((parts,)),
            pltpu.SemaphoreType.DMA((parts, 2)),
        ],
        compiler_params=params(61),
        cost_estimate=cost(4_000_000_000, 8 << 20),
    )(weight)


def project_kernel(half, a_own, a_far, w_own, w_far, *refs):
    outs, bounds = refs[-1 - len(SUMS) : -1], refs[-1]
    tile = pl.program_id(0)
    wide = TILE // 128
    count = HALF // TILE

    @pl.when(tile == 0)
    def _():
        for side, a_ref in enumerate((a_own, a_far)):
            limits = a_ref[:, 256:].astype(F32) * F32(math.sqrt(128.0))
            for i in range(count):
                at = (half * count + i) * wide
                bounds[i, side] = limits[:, at : at + wide]

    for at in range(0, TILE, 256):
        terms = []
        for side, (a_ref, w_ref) in enumerate(((a_own, w_own), (a_far, w_far))):
            term = jnp.dot(
                a_ref[:, :256],
                w_ref[:, at : at + 256],
                preferred_element_type=F32,
            )
            for part in range(2):
                lane = at // 128 + part
                limit = jnp.broadcast_to(bounds[tile, side, :, lane : lane + 1], (256, 128))
                kept = term[:, part * 128 : part * 128 + 128]
                terms.append(jnp.maximum(jnp.minimum(kept, limit), -limit))
        total = jnp.concatenate([terms[0] + terms[2], terms[1] + terms[3]], axis=1)
        row = 0
        for o_ref in outs:
            count_rows = o_ref.shape[0]
            o_ref[:, at : at + 256] = total[row : row + count_rows].astype(BF16)
            row += count_rows


def project(half, a_own, a_far, w_own, w_far, sums=None):
    first = half * (HALF // TILE)
    here = pl.BlockSpec((256, TILE), lambda i: (0, i))
    shapes = [(count, HALF if at == SPLIT else D) for at, count in enumerate(SUMS)]
    maps = [
        (lambda i: (0, i)) if at == SPLIT else (lambda i: (0, i + first))
        for at in range(len(SUMS))
    ]
    given = [] if sums is None else [x for at, x in enumerate(sums) if at != SPLIT]
    into = [at for at in range(len(SUMS)) if at != SPLIT]
    return pl.pallas_call(
        functools.partial(project_kernel, half),
        out_shape=tuple(jax.ShapeDtypeStruct(s, BF16) for s in shapes),
        grid=(HALF // TILE,),
        in_specs=[
            pl.BlockSpec((256, A_COLS), lambda i: (0, 0)),
            pl.BlockSpec((256, A_COLS), lambda i: (0, 0)),
            here,
            here,
        ]
        + [ANY] * len(given),
        out_specs=tuple(pl.BlockSpec((s[0], TILE), m) for s, m in zip(shapes, maps)),
        scratch_shapes=[pltpu.VMEM((HALF // TILE, 2, 256, TILE // 128), F32)],
        input_output_aliases={4 + i: into[i] for i in range(len(given))},
        compiler_params=params(24),
        cost_estimate=cost(4_000_000_000, 6_500_000),
    )(a_own, a_far, w_own, w_far, *given)


def step_kernel(body, n_in, *refs):
    ins, outs, token = refs[:n_in], refs[n_in + 1 : -1], refs[-1]
    values = body(*[r[...].astype(F32) for r in ins])
    for o_ref, value in zip(outs, values):
        o_ref[...] = value.astype(o_ref.dtype)
    token[...] = jnp.zeros((8, 128), F32)


def stage(body, ins, outs, token, span=15):
    *results, token = pl.pallas_call(
        functools.partial(step_kernel, body, len(ins)),
        out_shape=tuple(jax.ShapeDtypeStruct(s, BF16) for s in outs) + (TOKEN,),
        in_specs=[VMEM] * len(ins) + [ANY],
        out_specs=(VMEM,) * (len(outs) + 1),
        compiler_params=params(24),
        cost_estimate=cost(span * 1_150_000_000, span * 3_600_000),
    )(*ins, token)
    return results, token


def finish(total, residual, gain):
    stacked = jnp.concatenate([total[:, b * 128 : b * 128 + 128] for b in range(64)], axis=0)
    table = sylvester(128)
    high = stacked.astype(BF16)
    low = (stacked - high.astype(F32)).astype(BF16)
    turned = jnp.dot(high, table, preferred_element_type=F32)
    turned = turned + jnp.dot(low, table, preferred_element_type=F32)
    turned = turned * F32(1.0 / 128.0)
    mixed = jnp.concatenate([turned[b * 8 : b * 8 + 8] for b in range(64)], axis=1)
    updated = residual + mixed
    inverse = lax.rsqrt(jnp.mean(updated * updated, axis=1, keepdims=True) + 1e-05)
    return updated * inverse * gain, updated


def halves(both, half_down, half_up):
    rows = half_down.shape[0]
    down, up = both[:rows], both[rows:]
    down = jnp.concatenate([down[:, :HALF] + half_down, down[:, HALF:]], axis=1)
    up = jnp.concatenate([up[:, :HALF], up[:, HALF:] + half_up], axis=1)
    return down, up


def times(x_refs, w_ref):
    total = None
    for at in range(0, D, 1024):
        rows = jnp.concatenate([x[:, at : at + 1024].astype(F32) for x in x_refs], axis=0)
        part = jnp.dot(
            rows.astype(BF16), w_ref[at : at + 1024, :], preferred_element_type=F32
        )
        total = part if total is None else total + part
    return total


def next_kernel(*refs):
    *x_refs, w_ref, _, o_ref, token = refs
    token[...] = jnp.zeros((8, 128), F32)
    o_ref[...] = times(x_refs, w_ref).astype(BF16)


def next_rows(chunks, weight, token):
    count = sum(x.shape[0] for x in chunks)
    return pl.pallas_call(
        next_kernel,
        out_shape=(jax.ShapeDtypeStruct((count, 256), BF16), TOKEN),
        in_specs=[VMEM] * (len(chunks) + 1) + [ANY],
        out_specs=(VMEM, VMEM),
        compiler_params=params(24),
        cost_estimate=cost(2 * count * D * 256, (4 << 20) + count * 16384),
    )(*chunks, weight, token)


def last_kernel(n_rows, n_groups, meta, code_ref, *refs):
    groups, x_refs = refs[:n_groups], refs[n_groups : n_groups + 1]
    w_ref, o_ref = refs[n_groups + 1], refs[-1]
    code = code_ref[...]
    target = placed(code & 255, meta[0], meta[1], (code >> 8) ^ meta[2])
    to = lax.broadcasted_iota(jnp.int32, (512, n_rows), 0)
    pick = (target == to).astype(F32).astype(BF16)
    rows = [x[...] for x in groups] + [times(x_refs, w_ref).astype(BF16)]
    rows = jnp.concatenate([x.astype(F32) for x in rows], axis=0).astype(BF16)
    value = jnp.dot(pick, rows, preferred_element_type=F32)
    if len(refs) > n_groups + 3:
        value = value + refs[n_groups + 2][...]
    o_ref[...] = value.astype(o_ref.dtype)


def last_rows(meta, codes, groups, chunk, weight, *sofar):
    table = np.array(codes, np.int32).reshape(1, -1)
    count = table.shape[1]
    return pl.pallas_call(
        functools.partial(last_kernel, count, len(groups)),
        out_shape=jax.ShapeDtypeStruct((512, 256), BF16 if sofar else F32),
        in_specs=[pl.BlockSpec(memory_space=pltpu.SMEM)]
        + [VMEM] * (len(groups) + 3 + len(sofar)),
        out_specs=VMEM,
        compiler_params=params(24),
        cost_estimate=cost(1_000_000_000, 6 << 20),
    )(meta, jnp.asarray(table), *groups, chunk, weight, *sofar)


def local(
    query, keys, values, out_weight, scale_exp, residual, norm_gain, next_weight, doc_lengths
):
    rank = lax.axis_index("tensor")
    meta = jnp.stack([rank >> 4, (rank >> 1) & 7, rank & 1, rank >> 2]).astype(jnp.int32)
    expo = scale_exp[0].T
    w_own = turn(out_weight)
    w_far = [send(w, C_SWAP) for w in w_own]
    given = (meta, doc_lengths, query, expo, keys, values)
    a_far = send(attend(1, *given), C_SWAP)
    a_own = attend(0, *given)
    sums = project(0, a_own, a_far, w_own[0], w_far[0])
    q_down = sums[SPLIT]
    sums = project(1, a_own, a_far, w_own[1], w_far[1], sums)
    *p_sends, p_own, q_up = sums[:5]
    p_owns, q_owns = sums[5:9], sums[9:13]
    gain = norm_gain.reshape(1, -1)

    token = jnp.zeros((8, 128), F32)
    q_down, q_up = send(q_down, Z_DOWN), send(q_up, Z_UP)
    p_got, p_mid = send(p_sends[0], Y_SWAP), send(p_sends[1], Y_SWAP)
    (p_down, p_up), token = stage(
        lambda a, b: ((a + b)[:, :HALF], (a + b)[:, HALF:]),
        (p_own, p_got),
        ((8, HALF), (8, HALF)),
        token,
    )
    p_down, p_up = send(p_down, Z_DOWN), send(p_up, Z_UP)
    for step in range(3):
        if step == 0:
            q_body = halves
            p_body = lambda a, b, d, u: halves(a + b[:16], d, u)
        else:
            q_body = lambda a, d, u: (a[:16] + d, a[16:] + u)
            at = 16 if step == 1 else 0
            p_body = lambda a, b, d, u, at=at: (
                a[:8] + b[at : at + 8] + d,
                a[8:] + b[at + 8 : at + 16] + u,
            )
        (q_down, q_up), token = stage(
            q_body, (q_owns[step], q_down, q_up), ((16, D), (16, D)), token
        )
        q_down, q_up = send(q_down, Z_DOWN), send(q_up, Z_UP)
        (p_down, p_up), token = stage(
            p_body,
            (p_owns[step], p_mid if step < 2 else p_rest, p_down, p_up),
            ((8, D), (8, D)),
            token,
        )
        if step == 0:
            later, p_down = lax.optimization_barrier((p_sends[2], p_down))
            p_rest = send(later, Y_SWAP)
        if step == 2:
            own_residual, p_down = lax.optimization_barrier((residual[8:], p_down))
            far_residual = send(own_residual, Y_SWAP)
        p_down, p_up = send(p_down, Z_DOWN), send(p_up, Z_UP)
    (q_sum,), token = stage(
        lambda a, d, u: (a + d + u,), (q_owns[3], q_down, q_up), ((16, D),), token
    )
    q_got = send(q_sum, Y_SWAP)
    (p_norm, p_updated), token = stage(
        lambda a, b, d, u, r, g: finish(a + b[16:] + d + u, r, g),
        (p_owns[3], p_rest, p_down, p_up, residual[:8], gain),
        ((8, D), (8, D)),
        token,
    )
    def finish_pair(a, b, r, far_r, g):
        near, updated = finish(a[:8] + b[8:], r, g)
        far, _ = finish(a[8:] + b[:8], far_r, g)
        return jnp.concatenate([near, far], axis=0), updated

    (q_pair, q_updated), token = stage(
        finish_pair,
        (q_sum, q_got, residual[8:], far_residual, gain),
        ((16, D), (8, D)),
        token,
    )

    groups, codes = [], []

    def multiply(chunks, token):
        rows, token = next_rows([x for x, _ in chunks], next_weight, token)
        groups.append(rows)
        for _, code in chunks:
            codes.extend(code)
        return token

    def cores(value, code):
        return [(value, code), (send(value, C_SWAP), [256 + v for v in code])]

    def rows(piece, far, *chips):
        return [v for k in chips for ky in far for v in row_code(piece, k, ky)]

    def stack(*parts):
        return jnp.concatenate(parts, axis=0)

    p_up, p_down = send(p_norm, Z_UP), send(p_norm, Z_DOWN)
    q_up, q_down = send(q_pair, Z_UP), send(q_pair, Z_DOWN)
    p_held, p_held_chips = (p_norm,), (0,)
    q_held, q_held_code = (q_pair,), rows(1, (0, 1), 0)
    ready = None
    for hop in range(1, 4):
        chips = (8 - hop, hop)
        count = 8 * len(p_held) + 16
        (p_up, p_down, p_both), token = stage(
            lambda u, d, *h: (u, d, stack(*h, u, d)),
            (p_up, p_down, *p_held),
            ((8, D), (8, D), (count, D)),
            token,
        )
        if hop == 1:
            (updated,), token = stage(
                lambda a, b: (stack(a, b),), (p_updated, q_updated), ((16, D),), token, 1
            )
        p_chips = p_held_chips + chips
        if hop < 3:
            p_up, p_down = send(p_up, Z_UP), send(p_down, Z_DOWN)
        else:
            p_up, p_down = send(p_up[:, :HALF], Z_UP), send(p_down[:, HALF:], Z_DOWN)
        p_far = send(p_both, Y_SWAP)
        if ready is not None:
            token = multiply(ready, token)
        whole = (p_both, *q_held)
        (q_up, q_down, packed), token = stage(
            lambda u, d, *h: (u, d, stack(*h, u, d)),
            (q_up, q_down, *whole),
            ((16, D), (16, D), (32 + sum(x.shape[0] for x in whole), D)),
            token,
        )
        code = rows(0, (0,), *p_chips) + q_held_code + rows(1, (0, 1), *chips)
        if hop < 3:
            q_up, q_down = send(q_up, Z_UP), send(q_down, Z_DOWN)
        else:
            q_up, q_down = send(q_up[:, :HALF], Z_UP), send(q_down[:, HALF:], Z_DOWN)
        ready = cores(packed, code)
        q_held, q_held_code = (p_far,), rows(0, (1,), *p_chips)
        p_held, p_held_chips = (), ()
    (p_last,), token = stage(
        lambda u, d: (jnp.concatenate([u, d], axis=1),), (p_up, p_down), ((8, D),), token
    )
    p_far = send(p_last, Y_SWAP)
    token = multiply(ready, token)
    (packed,), token = stage(
        lambda u, d, *h: (stack(*h, jnp.concatenate([u, d], axis=1)),),
        (q_up, q_down, p_last, *q_held, p_far),
        ((48, D),),
        token,
        1,
    )
    code = rows(0, (0,), 4) + q_held_code + rows(0, (1,), 4) + rows(1, (0, 1), 4)
    (_, near), (swapped, far) = cores(packed, code)
    sofar = last_rows(meta, codes + near, groups, packed, next_weight)
    return last_rows(meta, far, [], swapped, next_weight, sofar), updated


def solution(mesh):
    return jax.shard_map(
        local,
        mesh=mesh,
        in_specs=(
            P("dp", "tensor"),
            P("dp", None),
            P("dp", None),
            P("tensor", None),
            P("tensor", "dp", None),
            P(("dp", "tensor"), None),
            P(),
            P(None, "tensor"),
            P("dp"),
        ),
        out_specs=(P("dp", "tensor"), P(("dp", "tensor"), None)),
        check_vma=False,
    )
```
